512 devices in a mesh: scen: 16 (over y, x_lo, core), row: 32 (over z, x_hi).
Axes of the slice: x: 4 (x_hi: 2, x_lo: 2; x = x_hi * 2 + x_lo), y: 4, z: 16, core: 2. Of those that a mesh axis runs over, the one named last changes fastest.
Arguments:
- borders: bfloat16 [16, 1024, 12288], P('scen', None, 'row'), may hold values from -1.078125 to 1.078125
- kkt_inverse: bfloat16 [16, 1024, 1024], P('scen', 'row'), may hold values from -0.35 to 2.35, as said below
- first_section: float32 [12288, 256], P('row'), may hold values from -6 to 6
- barrier: float32 [12288], P('row'), may hold values from 64 to 512
- panel_vars: int32 [256], replicated, may hold values from 0 to 12287, as said below
- probability: float32 [16], replicated, may hold values from 0.5 to 2
- assignment: int32 [16], P('scen'), may hold values from 0 to 15, each once
Outputs:
- factor: float32 [12288, 256], P('row')
The draws below stay inside these ranges and needn't reach their ends.
Inputs may be any that keep to these rules, and one draw needn't show every extreme that they name: `panel_vars`: distinct values. `kkt_inverse`: each scenario's matrix is symmetric positive definite. `assignment`: each scenario once.
All inputs are finite; a program needn't handle non-finite values.
Results may differ from the reference program's by a relative error of at most 0.00031.
Values may be sent and summed in bfloat16 or wider, within the bound.
No kernel may reach another device: no remote copies, remote signals or barrier semaphores. Data moves between devices by JAX's collectives and lax.ppermute only.
A program may use at most 64 MiB of HBM per device.

```python
import math
import jax
import jax.numpy as jnp
from jax import lax

N0 = 12288
NS = 1024
PANEL = 128
PANELS = 2
WIN = 256
SCENARIOS = 16


def draw_panel_vars(key, part):
    chosen = jax.random.permutation(jax.random.fold_in(key, 11), N0)
    return chosen[:WIN].astype(jnp.int32)


def draw_kkt_inverse(key, part):
    noise_key, diag_key = jax.random.split(jax.random.fold_in(key, 23))
    noise = jnp.clip(jax.random.normal(noise_key, (SCENARIOS, NS, NS), jnp.float32), -3.0, 3.0)
    symmetric = (noise + jnp.swapaxes(noise, 1, 2)) * (0.4 / math.sqrt(2.0 * NS))
    diagonal = jnp.exp(jax.random.uniform(diag_key, (SCENARIOS, NS), jnp.float32, 0.0, math.log(2.0)))
    result = symmetric + diagonal[:, :, None] * jnp.eye(NS, dtype=jnp.float32)[None, :, :]
    return result.astype(jnp.bfloat16)


def levels(rng, extent, cuts, smallest, high):
    def one(position, parts):
        draws = jax.random.uniform(jax.random.fold_in(jax.random.fold_in(rng, 6), position), (parts,), jnp.float32, smallest / len(cuts), high / len(cuts))
        return jnp.repeat(jnp.exp(draws), extent[position] // parts).reshape((-1,) + (1,) * (len(extent) - position - 1))

    level = one(*cuts[0])
    for cut in cuts[1:]:
        level = level * one(*cut)
    return level


def normal_values(rng, extent, deviation, reach, pieces=(), kind=jnp.bfloat16):
    loudness = levels(rng, extent, pieces, -0.22, 0.18) if pieces else 1.0
    entries = jax.random.normal(rng, extent, jnp.float32) * deviation * loudness
    return jnp.minimum(jnp.maximum(entries, -reach), reach).astype(kind)


def setup_inputs(seed: int = 0) -> dict:
    streams_of = jax.random.split(jax.random.key(seed), 8)
    return {
        "borders": normal_values(streams_of[0], (SCENARIOS, NS, N0), 0.18, 1.078125, ((0, 16), (2, 32))),
        "kkt_inverse": draw_kkt_inverse(jax.random.fold_in(streams_of[7], 71), 0),
        "first_section": normal_values(streams_of[2], (N0, WIN), 1.0, 6.0, ((0, 32),), jnp.float32),
        "barrier": jnp.clip(jnp.exp(math.log(512.0) - 2.0794415 * jax.random.uniform(streams_of[3], (N0,), jnp.float32) ** levels(streams_of[3], (N0,), ((0, 32),), -0.2, 0.2)), 64.0, 512.0),
        "panel_vars": draw_panel_vars(jax.random.fold_in(streams_of[7], 71), 0),
        "probability": jnp.clip(jnp.exp(jax.random.uniform(streams_of[5], (SCENARIOS,), jnp.float32, math.log(0.5), math.log(2.0))), 0.5, 2.0),
        "assignment": jax.random.permutation(streams_of[6], SCENARIOS).astype(jnp.int32),
    }


def factorize(diag_block, row_block):
    symmetric = 0.5 * (diag_block + diag_block.T)
    block_parts = []
    row_parts = []
    for panel_index in range(PANELS):
        low_col = panel_index * PANEL
        high_col = low_col + PANEL
        block_cols = symmetric[:, low_col:high_col]
        row_cols = row_block[:, low_col:high_col]
        if panel_index > 0:
            earlier_block = jnp.concatenate(block_parts, axis=1)
            earlier_rows = jnp.concatenate(row_parts, axis=1)
            across = earlier_block[low_col:high_col, :]
            block_cols = block_cols - jnp.dot(earlier_block, across.T, precision=lax.Precision.HIGHEST)
            row_cols = row_cols - jnp.dot(earlier_rows, across.T, precision=lax.Precision.HIGHEST)
        panel_chol = jnp.linalg.cholesky(block_cols[low_col:high_col, :])
        block_parts.append(lax.linalg.triangular_solve(panel_chol, block_cols, left_side=False, lower=True, transpose_a=True))
        row_parts.append(lax.linalg.triangular_solve(panel_chol, row_cols, left_side=False, lower=True, transpose_a=True))
    return jnp.concatenate(row_parts, axis=1)

def reference(borders, kkt_inverse, first_section, barrier, panel_vars, probability, assignment):
    scen_count = borders.shape[0]
    picked = jnp.take(borders, panel_vars, axis=2)
    weights = jnp.take(probability, assignment)

    def accumulate(scen_index, total):
        inverse = lax.dynamic_index_in_dim(kkt_inverse, scen_index, 0, keepdims=False)
        columns = lax.dynamic_index_in_dim(picked, scen_index, 0, keepdims=False)
        border = lax.dynamic_index_in_dim(borders, scen_index, 0, keepdims=False)
        solved = jnp.dot(inverse.astype(jnp.float32), columns.astype(jnp.float32), preferred_element_type=jnp.float32).astype(jnp.bfloat16)
        term = lax.dot_general(border.astype(jnp.float32), solved.astype(jnp.float32), (((0,), (0,)), ((), ())), preferred_element_type=jnp.float32)
        return total + weights[scen_index] * term
    total = lax.fori_loop(0, scen_count, accumulate, jnp.zeros((N0, WIN), jnp.float32))
    hits = jnp.arange(N0, dtype=jnp.int32)[:, None] == panel_vars[None, :]
    schur = total + first_section + jnp.where(hits, barrier[:, None], jnp.zeros((), jnp.float32))
    diag_block = jnp.take(schur, panel_vars, axis=0)
    return factorize(diag_block, schur)
```

```python
import jax
import jax.numpy as jnp
from jax import lax
from jax.sharding import Mesh
from jax.sharding import PartitionSpec as P

PANEL = 128
PANELS = 2
SLOTS = 24
ROW = ("z", "xh")
HIGHEST = lax.Precision.HIGHEST


def split_in_three(x):
    high = x.astype(jnp.bfloat16)
    rest = x - high.astype(jnp.float32)
    middle = rest.astype(jnp.bfloat16)
    low = (rest - middle.astype(jnp.float32)).astype(jnp.bfloat16)
    return high, middle, low


def from_everyone(x, axis):
    copies = jnp.broadcast_to(x, (lax.axis_size(axis), *x.shape))
    return lax.all_to_all(copies, axis, split_axis=0, concat_axis=0, tiled=True)


def swapped(x):
    return lax.ppermute(x, "xh", [(0, 1), (1, 0)])


def factorize(diag_block, row_block):
    symmetric = 0.5 * (diag_block + diag_block.T)
    block_parts = []
    row_parts = []
    for panel_index in range(PANELS):
        low_col = panel_index * PANEL
        high_col = low_col + PANEL
        block_cols = symmetric[:, low_col:high_col]
        row_cols = row_block[:, low_col:high_col]
        if panel_index > 0:
            earlier_block = block_parts[0]
            earlier_rows = row_parts[0]
            across = earlier_block[low_col:high_col, :]
            block_cols = block_cols - jnp.dot(earlier_block, across.T, precision=HIGHEST)
            row_cols = row_cols - jnp.dot(earlier_rows, across.T, precision=HIGHEST)
        panel_chol = jnp.linalg.cholesky(block_cols[low_col:high_col, :])
        block_parts.append(
            lax.linalg.triangular_solve(
                panel_chol, block_cols, left_side=False, lower=True, transpose_a=True
            )
        )
        row_parts.append(
            lax.linalg.triangular_solve(
                panel_chol, row_cols, left_side=False, lower=True, transpose_a=True
            )
        )
    return jnp.concatenate(row_parts, axis=1)


def per_device(borders, kkt_inverse, first_section, barrier, panel_vars, probability, assignment):
    border, inverse_rows = borders[0], kkt_inverse[0]
    rows_dev, win = first_section.shape
    z_count, scen_count = lax.axis_size("z"), lax.axis_size("scen")
    rows_inv = inverse_rows.shape[0]
    me_xh = lax.axis_index("xh")
    me_row = lax.axis_index("z") * 2 + me_xh
    me_scen = lax.axis_index("scen")

    other_rows = swapped(inverse_rows)
    first_half = jnp.where(me_xh == 0, inverse_rows, other_rows)
    second_half = jnp.where(me_xh == 0, other_rows, inverse_rows)
    inverse_pair = jnp.concatenate([first_half, second_half], axis=0)

    owner = panel_vars // rows_dev
    local = panel_vars - owner * rows_dev
    same = (owner[:, None] == owner[None, :]) & (jnp.arange(win)[:, None] > jnp.arange(win)[None, :])
    rank = jnp.sum(same.astype(jnp.int32), axis=1)
    rounds = jnp.max(rank) // SLOTS + 1

    def gather_round(turn):
        place = rank - turn * SLOTS
        slot = jnp.arange(SLOTS, dtype=jnp.int32)
        mine = (owner[None, :] == me_row) & (place[None, :] == slot[:, None])
        source = jnp.sum(jnp.where(mine, local[None, :] + 1, 0), axis=1) - 1
        pick = (source[:, None] == jnp.arange(rows_dev)[None, :]).astype(jnp.bfloat16)
        picked = lax.dot_general(
            pick, border, (((1,), (1,)), ((), ())), preferred_element_type=jnp.float32
        ).astype(jnp.bfloat16)
        everyone = lax.all_gather(picked, "z", axis=0, tiled=True)
        holder = jnp.arange(z_count * SLOTS, dtype=jnp.int32)
        put = (owner[None, :] == (holder // SLOTS * 2 + me_xh)[:, None]) & (
            place[None, :] == (holder % SLOTS)[:, None]
        )
        return lax.dot_general(
            everyone,
            put.astype(jnp.bfloat16),
            (((0,), (0,)), ((), ())),
            preferred_element_type=jnp.float32,
        ).astype(jnp.bfloat16)

    half_columns = gather_round(jnp.int32(0))
    _, half_columns = lax.while_loop(
        lambda state: state[0] < rounds,
        lambda state: (state[0] + 1, state[1] + gather_round(state[0])),
        (jnp.int32(1), half_columns),
    )
    columns = half_columns + swapped(half_columns)

    share = win // scen_count
    share_vars = lax.dynamic_slice(panel_vars, (me_scen * share,), (share,)) - me_row * rows_dev
    held = (share_vars >= 0) & (share_vars < rows_dev)
    at = jnp.clip(share_vars, 0, rows_dev - 1)
    window_place = me_scen * share + jnp.arange(share, dtype=jnp.int32)
    on_diagonal = window_place[:, None] == jnp.arange(win, dtype=jnp.int32)[None, :]
    base = jnp.take(first_section, at, axis=0) + jnp.where(
        on_diagonal, jnp.take(barrier, at)[:, None], 0.0
    )
    base = jnp.where(held[:, None], base, 0.0)

    own_solved = jnp.dot(inverse_pair, half_columns, preferred_element_type=jnp.float32)
    message = jnp.concatenate([own_solved.astype(jnp.bfloat16), *split_in_three(base)], axis=0)
    both = lax.all_gather(message, "xh", axis=0)
    message = both[0] + both[1]
    gathered = lax.all_gather(message, "z", axis=0)
    solved = gathered[:, : 2 * rows_inv].reshape(-1, win)
    parts = jnp.sum(gathered[:, 2 * rows_inv :].astype(jnp.float32), axis=0)
    base_share = parts[:share] + parts[share : 2 * share] + parts[2 * share :]

    matches = assignment[:, None] == jnp.arange(scen_count, dtype=jnp.int32)[None, :]
    weight = jnp.sum(jnp.where(matches, probability[None, :], 0.0))

    block_term = weight * lax.dot_general(
        columns, solved, (((0,), (0,)), ((), ())), preferred_element_type=jnp.float32
    )
    block_shares = lax.all_to_all(
        block_term.reshape(scen_count, share, win), "scen", 0, 0, tiled=True
    )
    block_share = jnp.sum(block_shares, axis=0) + base_share
    diag_block = from_everyone(block_share, "scen").reshape(win, win)

    term = weight * lax.dot_general(
        border, solved, (((0,), (0,)), ((), ())), preferred_element_type=jnp.float32
    )
    term_shares = lax.all_to_all(
        term.reshape(scen_count, rows_dev // scen_count, win), "scen", 0, 0, tiled=True
    )
    term_share = jnp.sum(term_shares, axis=0)
    total = from_everyone(term_share, "scen").reshape(rows_dev, win)
    hits = (
        jnp.arange(rows_dev, dtype=jnp.int32)[:, None] + me_row * rows_dev == panel_vars[None, :]
    )
    rows = total + first_section + jnp.where(hits, barrier[:, None], 0.0)
    return factorize(diag_block, rows)


def solution(mesh):
    torus = Mesh(mesh.devices.reshape(mesh.shape["scen"], 16, 2), ("scen", "z", "xh"))
    return jax.shard_map(
        per_device,
        mesh=torus,
        in_specs=(
            P("scen", None, ROW),
            P("scen", ROW, None),
            P(ROW, None),
            P(ROW),
            P(),
            P(),
            P("scen"),
        ),
        out_specs=P(ROW, None),
        check_vma=False,
    )
```

```python
import jax
import jax.numpy as jnp
from jax import lax
from jax.experimental import pallas as pl
from jax.experimental.pallas import tpu as pltpu
from jax.sharding import Mesh
from jax.sharding import PartitionSpec as P

SLOTS = 24
GROUP = 8
PANEL = 128
ROW = ("z", "xh")
HIGHEST = lax.Precision.HIGHEST
F32 = jnp.float32
BF16 = jnp.bfloat16
LIMIT = pltpu.CompilerParams(vmem_limit_bytes=48 * 1024 * 1024)


def iota(shape, dim):
    return lax.broadcasted_iota(jnp.int32, shape, dim)


def contract(a, b, dim_a, dim_b, precision=None):
    return lax.dot_general(
        a, b, (((dim_a,), (dim_b,)), ((), ())), precision=precision, preferred_element_type=F32
    )


def from_everyone(x, axis):
    copies = jnp.broadcast_to(x, (lax.axis_size(axis), *x.shape))
    return lax.all_to_all(copies, axis, split_axis=0, concat_axis=0, tiled=True)


def swapped(x):
    return lax.ppermute(x, "xh", [(0, 1), (1, 0)])


def places(panel_row, rows_dev, holders):
    win = panel_row.shape[1]
    owner = jnp.zeros_like(panel_row)
    for holder in range(1, holders):
        owner = owner + (panel_row >= holder * rows_dev).astype(jnp.int32)
    across = jnp.broadcast_to(owner, (win, win))
    earlier, later = iota((win, win), 0), iota((win, win), 1)
    down = jnp.sum(jnp.where(earlier == later, across, 0), axis=1, keepdims=True)
    same = (across == down) & (earlier < later)
    rank = jnp.sum(same.astype(jnp.int32), axis=0, keepdims=True)
    return owner, rank


def pick_kernel(holders, turn_ref, panel_ref, border_ref, picked_ref, put_ref, rounds_ref):
    rows_dev = border_ref.shape[1]
    z_count = put_ref.shape[0] // SLOTS
    xh = lax.axis_index("xh")
    me = lax.axis_index("z") * 2 + xh
    panel_row = panel_ref[...]
    owner, rank = places(panel_row, rows_dev, holders)
    rounds_ref[0] = jnp.max(rank) + 1
    win = panel_row.shape[1]
    place = rank - turn_ref[0] * SLOTS
    slot = iota((SLOTS, win), 0)
    in_slot = place == slot
    mine = in_slot & (owner == me)
    local = panel_row - me * rows_dev
    source = jnp.sum(jnp.where(mine, local + 1, 0), axis=1, keepdims=True) - 1
    pick = (source == iota((SLOTS, rows_dev), 1)).astype(F32).astype(BF16)
    picked_ref[...] = contract(pick, border_ref[...], 1, 1).astype(BF16)
    put = [
        jnp.where(in_slot & (owner == 2 * holder + xh), 1.0, 0.0) for holder in range(z_count)
    ]
    put_ref[...] = jnp.concatenate(put, axis=0).astype(BF16)


def gather_round(turn, panel_row, border):
    rows_inv, rows_dev = border.shape
    win = panel_row.shape[1]
    z_count = lax.axis_size("z")
    vmem = pl.BlockSpec(memory_space=pltpu.VMEM)
    smem = pl.BlockSpec(memory_space=pltpu.SMEM)
    picked, put, most = pl.pallas_call(
        lambda *refs: pick_kernel(2 * z_count, *refs),
        out_shape=(
            jax.ShapeDtypeStruct((SLOTS, rows_inv), BF16),
            jax.ShapeDtypeStruct((z_count * SLOTS, win), BF16),
            jax.ShapeDtypeStruct((1,), jnp.int32),
        ),
        in_specs=[smem, vmem, vmem],
        out_specs=(vmem, vmem, smem),
        compiler_params=LIMIT,
    )(turn, panel_row, border)
    everyone = lax.all_gather(picked, "z", axis=0, tiled=True)
    return contract(everyone, put, 0, 0).astype(BF16), most[0]


def solve_kernel(own_ref, other_ref, half_ref, panel_ref, barrier_ref, first_ref, out_ref):
    rows_inv = own_ref.shape[0]
    rows_dev, win = first_ref.shape
    xh = lax.axis_index("xh")
    me = lax.axis_index("z") * 2 + xh
    share = win // lax.axis_size("scen")
    half = half_ref[...]
    own = contract(own_ref[...], half, 1, 0)
    other = contract(other_ref[...], half, 1, 0)
    low = jnp.where(xh == 0, own, other)
    high = jnp.where(xh == 0, other, own)
    place = lax.axis_index("scen") * share + iota((share, win), 0)
    on_diagonal = place == iota((share, win), 1)
    local = jnp.sum(jnp.where(on_diagonal, panel_ref[...], 0), axis=1, keepdims=True) - me * rows_dev
    hit = local == iota((share, rows_dev), 1)
    pick = hit.astype(F32)
    base = contract(pick, first_ref[...], 1, 0, HIGHEST)
    term = jnp.sum(jnp.where(hit, barrier_ref[...], 0.0), axis=1, keepdims=True)
    base = base + jnp.where(on_diagonal, term, 0.0)
    first = base.astype(BF16).astype(F32)
    second = (base - first).astype(BF16).astype(F32)
    third = base - first - second
    out_ref[...] = jnp.concatenate([low, high, first, second, third], axis=0).astype(BF16)


def term_kernel(
    own_ref, other_ref, border_ref, gathered_ref, prob_ref, slot_ref, out_ref, base_ref
):
    z_count, lines, win = gathered_ref.shape
    rows_inv = border_ref.shape[0]
    rows_dev = border_ref.shape[1]
    scen_count, per_scen, _ = out_ref.shape
    share = win // scen_count
    step = rows_inv // z_count
    solved = gathered_ref[:, :step, :].reshape(rows_inv, win)
    match = iota(prob_ref.shape, 1) == slot_ref[...]
    weight = jnp.sum(jnp.where(match, prob_ref[...], 0.0), axis=1, keepdims=True)
    columns = own_ref[...] + other_ref[...]
    block = contract(columns, solved, 0, 0) * weight
    out_ref[:, :share, :] = block.reshape(scen_count, share, win)
    term = contract(border_ref[...], solved, 0, 0) * weight
    out_ref[:, share:, :] = term.reshape(scen_count, per_scen - share, win)
    parts = jnp.sum(gathered_ref[:, step:, :].astype(F32), axis=0)
    base_ref[...] = parts[:share] + parts[share : 2 * share] + parts[2 * share :]


def inverse_factor(symmetric):
    size = symmetric.shape[0]
    count = size // GROUP
    work = [symmetric[GROUP * i : GROUP * (i + 1), :] for i in range(count)]
    lane, sub = iota((GROUP, size), 1), iota((GROUP, size), 0)
    result = []
    for group in range(count):
        low = group * GROUP
        block = work[group]
        inside = (lane >= low) & (lane < low + GROUP)
        lower = [[None] * GROUP for _ in range(GROUP)]
        scale = [None] * GROUP
        entry = [
            [jnp.broadcast_to(block[i : i + 1, low + j : low + j + 1], block.shape) for j in range(i + 1)]
            for i in range(GROUP)
        ]
        for j in range(GROUP):
            pivot = entry[j][j]
            for t in range(j):
                pivot = pivot - lower[j][t] * lower[j][t]
            scale[j] = lax.rsqrt(pivot)
            for i in range(j + 1, GROUP):
                value = entry[i][j]
                for t in range(j):
                    value = value - lower[i][t] * lower[j][t]
                lower[i][j] = value * scale[j]
        forward = []
        for i in range(GROUP):
            row = jnp.broadcast_to(block[i : i + 1, :], block.shape)
            row = jnp.where(inside, jnp.where(lane == low + i, 1.0, 0.0), row)
            for j in range(i):
                row = row - lower[i][j] * forward[j]
            forward.append(row * scale[i])
        done = forward[0]
        for i in range(1, GROUP):
            done = jnp.where(sub == i, forward[i], done)
        result.append(jnp.where(lane <= sub + low, done, 0.0))
        if group + 1 == count:
            break
        back = [None] * GROUP
        for i in reversed(range(GROUP)):
            row = forward[i]
            for j in range(i + 1, GROUP):
                row = row - lower[j][i] * back[j]
            back[i] = row * scale[i]
        for later in range(group + 1, count):
            old = work[later]
            new = jnp.where(inside, 0.0, old)
            for j in range(GROUP):
                new = new - old[:, low + j : low + j + 1] * back[j]
            work[later] = new
    return jnp.concatenate(result, axis=0)


def factor_kernel(gathered_ref, base_ref, out_ref):
    scen_count, per_scen, win = gathered_ref.shape
    share = win // scen_count
    diag = gathered_ref[:, :share, :].reshape(win, win)
    rows = gathered_ref[:, share:, :].reshape(base_ref.shape) + base_ref[...]

    def symmetric(i, j):
        one = diag[i : i + PANEL, j : j + PANEL]
        other = diag[j : j + PANEL, i : i + PANEL]
        return 0.5 * (one + other.T)

    first = inverse_factor(symmetric(0, 0))
    across = contract(symmetric(PANEL, 0), first, 1, 1, HIGHEST)
    second = inverse_factor(symmetric(PANEL, PANEL) - contract(across, across, 1, 1, HIGHEST))
    left = contract(rows[:, :PANEL], first, 1, 1, HIGHEST)
    right = rows[:, PANEL:] - contract(left, across, 1, 1, HIGHEST)
    out_ref[:, :PANEL] = left
    out_ref[:, PANEL:] = contract(right, second, 1, 1, HIGHEST)


def per_device(borders, kkt_inverse, first_section, barrier, panel_vars, probability, assignment):
    border, inverse_rows = borders[0], kkt_inverse[0]
    rows_inv, rows_dev = border.shape
    win = first_section.shape[1]
    scen_count = lax.axis_size("scen")
    me_row = lax.axis_index("z") * 2 + lax.axis_index("xh")
    panel_row = panel_vars[None, :]

    other_rows = swapped(inverse_rows)
    half, most = gather_round(jnp.zeros((1,), jnp.int32), panel_row, border)
    _, half = lax.while_loop(
        lambda state: state[0] * SLOTS < most,
        lambda state: (
            state[0] + 1,
            state[1] + gather_round(state[0][None], panel_row, border)[0],
        ),
        (jnp.int32(1), half),
    )
    other_half = swapped(half)

    share = win // scen_count
    own_lines = 2 * inverse_rows.shape[0]
    message = pl.pallas_call(
        solve_kernel,
        out_shape=jax.ShapeDtypeStruct((own_lines + 3 * share, win), BF16),
        compiler_params=LIMIT,
    )(inverse_rows, other_rows, half, panel_row, barrier[None, :], first_section)
    both = lax.all_gather(message, "xh", axis=0)
    gathered = lax.all_gather(both[0] + both[1], "z", axis=0)

    per_scen = share + rows_dev // scen_count
    terms, base = pl.pallas_call(
        term_kernel,
        out_shape=(
            jax.ShapeDtypeStruct((scen_count, per_scen, win), F32),
            jax.ShapeDtypeStruct((share, win), F32),
        ),
        compiler_params=LIMIT,
    )(half, other_half, border, gathered, probability[None, :], assignment[None, :])
    shares = lax.all_to_all(terms, "scen", 0, 0, tiled=True)
    summed = jnp.sum(shares, axis=0) + jnp.pad(base, ((0, per_scen - share), (0, 0)))
    everyone = from_everyone(summed, "scen")

    hits = (
        jnp.arange(rows_dev, dtype=jnp.int32)[:, None] + me_row * rows_dev == panel_vars[None, :]
    )
    rows_base = first_section + jnp.where(hits, barrier[:, None], 0.0)
    return pl.pallas_call(
        factor_kernel,
        out_shape=jax.ShapeDtypeStruct((rows_dev, win), F32),
        compiler_params=LIMIT,
    )(everyone, rows_base)


def solution(mesh):
    torus = Mesh(mesh.devices.reshape(mesh.shape["scen"], 16, 2), ("scen", "z", "xh"))
    return jax.shard_map(
        per_device,
        mesh=torus,
        in_specs=(
            P("scen", None, ROW),
            P("scen", ROW, None),
            P(ROW, None),
            P(ROW),
            P(),
            P(),
            P("scen"),
        ),
        out_specs=P(ROW, None),
        check_vma=False,
    )
```

```python
import jax
import jax.numpy as jnp
from jax import lax
from jax.experimental import pallas as pl
from jax.experimental.pallas import tpu as pltpu
from jax.sharding import Mesh
from jax.sharding import PartitionSpec as P

SLOTS = 24
GROUP = 8
PANEL = 128
Z = ("zh", "zl")
ROW = ("zh", "zl", "xh")
FAR = ("zh", "xh")
HIGHEST = lax.Precision.HIGHEST
F32 = jnp.float32
BF16 = jnp.bfloat16
LIMIT = pltpu.CompilerParams(vmem_limit_bytes=48 * 1024 * 1024)


def iota(shape, dim):
    return lax.broadcasted_iota(jnp.int32, shape, dim)


def contract(a, b, dim_a, dim_b, precision=None):
    return lax.dot_general(
        a, b, (((dim_a,), (dim_b,)), ((), ())), precision=precision, preferred_element_type=F32
    )


def from_everyone(x, axis):
    copies = jnp.broadcast_to(x, (lax.axis_size(axis), *x.shape))
    return lax.all_to_all(copies, axis, split_axis=0, concat_axis=0, tiled=True)


def swapped(x):
    return lax.ppermute(x, "xh", [(0, 1), (1, 0)])


def places(panel_row, rows_dev, holders):
    win = panel_row.shape[1]
    owner = jnp.zeros_like(panel_row)
    for holder in range(1, holders):
        owner = owner + (panel_row >= holder * rows_dev).astype(jnp.int32)
    across = jnp.broadcast_to(owner, (win, win))
    earlier, later = iota((win, win), 0), iota((win, win), 1)
    down = jnp.sum(jnp.where(earlier == later, across, 0), axis=1, keepdims=True)
    same = (across == down) & (earlier < later)
    rank = jnp.sum(same.astype(jnp.int32), axis=0, keepdims=True)
    return owner, rank


def my_row():
    return (lax.axis_index("zh") * lax.axis_size("zl") + lax.axis_index("zl")) * 2 + lax.axis_index("xh")


def pick_kernel(holders, turn_ref, panel_ref, border_ref, picked_ref, put_ref, rounds_ref):
    rows_dev = border_ref.shape[1]
    z_count = put_ref.shape[0] // SLOTS
    xh = lax.axis_index("xh")
    me = my_row()
    panel_row = panel_ref[...]
    owner, rank = places(panel_row, rows_dev, holders)
    rounds_ref[0] = jnp.max(rank) + 1
    win = panel_row.shape[1]
    place = rank - turn_ref[0] * SLOTS
    slot = iota((SLOTS, win), 0)
    in_slot = place == slot
    mine = in_slot & (owner == me)
    local = panel_row - me * rows_dev
    source = jnp.sum(jnp.where(mine, local + 1, 0), axis=1, keepdims=True) - 1
    pick = (source == iota((SLOTS, rows_dev), 1)).astype(F32).astype(BF16)
    picked_ref[...] = contract(pick, border_ref[...], 1, 1).astype(BF16)
    put = [
        jnp.where(in_slot & (owner == 2 * holder + xh), 1.0, 0.0) for holder in range(z_count)
    ]
    put_ref[...] = jnp.concatenate(put, axis=0).astype(BF16)


def gather_round(turn, panel_row, border):
    rows_inv, rows_dev = border.shape
    win = panel_row.shape[1]
    z_count = lax.axis_size(Z)
    vmem = pl.BlockSpec(memory_space=pltpu.VMEM)
    smem = pl.BlockSpec(memory_space=pltpu.SMEM)
    picked, put, most = pl.pallas_call(
        lambda *refs: pick_kernel(2 * z_count, *refs),
        out_shape=(
            jax.ShapeDtypeStruct((SLOTS, rows_inv), BF16),
            jax.ShapeDtypeStruct((z_count * SLOTS, win), BF16),
            jax.ShapeDtypeStruct((1,), jnp.int32),
        ),
        in_specs=[smem, vmem, vmem],
        out_specs=(vmem, vmem, smem),
        compiler_params=LIMIT,
    )(turn, panel_row, border)
    everyone = lax.all_gather(picked, Z, axis=0, tiled=True)
    return contract(everyone, put, 0, 0).astype(BF16), most[0]


def base_kernel(panel_ref, barrier_ref, first_ref, inverse_ref, out_ref):
    copies, lines, rows_inv = out_ref.shape
    own = inverse_ref.shape[0]
    rows_dev, win = first_ref.shape
    share = win // lax.axis_size("scen")
    place = lax.axis_index("scen") * share + iota((share, win), 0)
    on_diagonal = place == iota((share, win), 1)
    local = jnp.sum(jnp.where(on_diagonal, panel_ref[...], 0), axis=1, keepdims=True)
    hit = local - my_row() * rows_dev == iota((share, rows_dev), 1)
    base = contract(hit.astype(F32), first_ref[...], 1, 0, HIGHEST)
    term = jnp.sum(jnp.where(hit, barrier_ref[...], 0.0), axis=1, keepdims=True)
    base = base + jnp.where(on_diagonal, term, 0.0)
    rounded = base.astype(BF16).astype(F32)
    rest = base - rounded
    fold = rows_inv // win
    step = share // fold
    lanes = [
        jnp.concatenate([part[step * i : step * (i + 1)] for i in range(fold)], axis=1)
        for part in (rounded, rest)
    ]
    message = jnp.concatenate([inverse_ref[...].astype(F32), *lanes], axis=0).astype(BF16)
    out_ref[...] = jnp.broadcast_to(message[None], out_ref.shape)


def solve_kernel(far_ref, half_ref, out_ref, base_ref):
    copies, lines, rows_inv = far_ref.shape
    win = half_ref.shape[1]
    extra = base_ref.shape[0] * win // rows_inv
    own = lines - extra
    far = far_ref[...].astype(F32)
    rows = far[:, :own, :].reshape(copies * own, rows_inv).astype(BF16)
    out_ref[...] = contract(rows, half_ref[...], 1, 0).astype(BF16)
    parts = jnp.sum(far[:, own:, :], axis=0)
    fold = rows_inv // win
    step = extra // 2
    lanes = [
        parts[step * p : step * (p + 1), win * i : win * (i + 1)] for p in range(2) for i in range(fold)
    ]
    base_ref[...] = jnp.concatenate(lanes, axis=0).astype(BF16)


def term_kernel(
    own_ref, other_ref, border_ref, gathered_ref, prob_ref, slot_ref, out_ref, base_ref, solved_ref
):
    near, lines, win = gathered_ref.shape
    rows_inv = border_ref.shape[0]
    scen_count, per_scen, _ = out_ref.shape
    share = win // scen_count
    held = rows_inv // near
    step = held // lax.axis_size("zh")
    for low in range(near):
        for high in range(held // step):
            at = (high * near + low) * step
            solved_ref[at : at + step, :] = gathered_ref[low, high * step : (high + 1) * step, :]
    solved = solved_ref[...]
    match = iota(prob_ref.shape, 1) == slot_ref[...]
    weight = jnp.sum(jnp.where(match, prob_ref[...], 0.0), axis=1, keepdims=True)
    columns = own_ref[...] + other_ref[...]
    block = contract(columns, solved, 0, 0) * weight
    out_ref[:, :share, :] = block.reshape(scen_count, share, win)
    term = contract(border_ref[...], solved, 0, 0) * weight
    out_ref[:, share:, :] = term.reshape(scen_count, per_scen - share, win)
    parts = jnp.sum(gathered_ref[:, held:, :].astype(F32), axis=0)
    base_ref[...] = parts[:share] + parts[share:]


def inverse_factor(symmetric):
    size = symmetric.shape[0]
    count = size // GROUP
    work = [symmetric[GROUP * i : GROUP * (i + 1), :] for i in range(count)]
    lane, sub = iota((GROUP, size), 1), iota((GROUP, size), 0)
    result = []
    for group in range(count):
        low = group * GROUP
        block = work[group]
        inside = (lane >= low) & (lane < low + GROUP)
        lower = [[None] * GROUP for _ in range(GROUP)]
        scale = [None] * GROUP
        entry = [
            [jnp.broadcast_to(block[i : i + 1, low + j : low + j + 1], block.shape) for j in range(i + 1)]
            for i in range(GROUP)
        ]
        for j in range(GROUP):
            pivot = entry[j][j]
            for t in range(j):
                pivot = pivot - lower[j][t] * lower[j][t]
            scale[j] = lax.rsqrt(pivot)
            for i in range(j + 1, GROUP):
                value = entry[i][j]
                for t in range(j):
                    value = value - lower[i][t] * lower[j][t]
                lower[i][j] = value * scale[j]
        forward = []
        for i in range(GROUP):
            row = jnp.broadcast_to(block[i : i + 1, :], block.shape)
            row = jnp.where(inside, jnp.where(lane == low + i, 1.0, 0.0), row)
            for j in range(i):
                row = row - lower[i][j] * forward[j]
            forward.append(row * scale[i])
        done = forward[0]
        for i in range(1, GROUP):
            done = jnp.where(sub == i, forward[i], done)
        result.append(jnp.where(lane <= sub + low, done, 0.0))
        if group + 1 == count:
            break
        back = [None] * GROUP
        for i in reversed(range(GROUP)):
            row = forward[i]
            for j in range(i + 1, GROUP):
                row = row - lower[j][i] * back[j]
            back[i] = row * scale[i]
        for later in range(group + 1, count):
            old = work[later]
            new = jnp.where(inside, 0.0, old)
            for j in range(GROUP):
                new = new - old[:, low + j : low + j + 1] * back[j]
            work[later] = new
    return jnp.concatenate(result, axis=0)


def factor_kernel(gathered_ref, base_ref, out_ref):
    scen_count, per_scen, win = gathered_ref.shape
    share = win // scen_count
    diag = gathered_ref[:, :share, :].reshape(win, win)
    rows = gathered_ref[:, share:, :].reshape(base_ref.shape) + base_ref[...]

    def symmetric(i, j):
        one = diag[i : i + PANEL, j : j + PANEL]
        other = diag[j : j + PANEL, i : i + PANEL]
        return 0.5 * (one + other.T)

    first = inverse_factor(symmetric(0, 0))
    across = contract(symmetric(PANEL, 0), first, 1, 1, HIGHEST)
    second = inverse_factor(symmetric(PANEL, PANEL) - contract(across, across, 1, 1, HIGHEST))
    left = contract(rows[:, :PANEL], first, 1, 1, HIGHEST)
    right = rows[:, PANEL:] - contract(left, across, 1, 1, HIGHEST)
    out_ref[:, :PANEL] = left
    out_ref[:, PANEL:] = contract(right, second, 1, 1, HIGHEST)


def per_device(borders, kkt_inverse, first_section, barrier, panel_vars, probability, assignment):
    border, inverse_rows = borders[0], kkt_inverse[0]
    rows_inv, rows_dev = border.shape
    win = first_section.shape[1]
    scen_count = lax.axis_size("scen")
    share = win // scen_count
    own_rows = inverse_rows.shape[0]
    panel_row = panel_vars[None, :]

    far_count = lax.axis_size(FAR)
    far_lines = own_rows + 2 * share * win // rows_inv
    far = pl.pallas_call(
        base_kernel,
        out_shape=jax.ShapeDtypeStruct((far_count, far_lines, rows_inv), BF16),
        compiler_params=LIMIT,
    )(panel_row, barrier[None, :], first_section, inverse_rows)
    far = lax.all_to_all(far, FAR, 0, 0, tiled=True)
    half, most = gather_round(jnp.zeros((1,), jnp.int32), panel_row, border)
    _, half = lax.while_loop(
        lambda state: state[0] * SLOTS < most,
        lambda state: (
            state[0] + 1,
            state[1] + gather_round(state[0][None], panel_row, border)[0],
        ),
        (jnp.int32(1), half),
    )

    solved, base = pl.pallas_call(
        solve_kernel,
        out_shape=(
            jax.ShapeDtypeStruct((far_count * own_rows, win), BF16),
            jax.ShapeDtypeStruct((2 * share, win), BF16),
        ),
        compiler_params=LIMIT,
    )(far, half)
    both = lax.all_gather(solved, "xh", axis=0)
    both, half = lax.optimization_barrier((both, half))
    other_half = swapped(half)
    message = jnp.concatenate([both[0] + both[1], base], axis=0)
    gathered = lax.all_gather(message, "zl", axis=0)

    per_scen = share + rows_dev // scen_count
    terms, base = pl.pallas_call(
        term_kernel,
        out_shape=(
            jax.ShapeDtypeStruct((scen_count, per_scen, win), F32),
            jax.ShapeDtypeStruct((share, win), F32),
        ),
        scratch_shapes=[pltpu.VMEM((rows_inv, win), BF16)],
        compiler_params=LIMIT,
    )(half, other_half, border, gathered, probability[None, :], assignment[None, :])
    shares = lax.all_to_all(terms, "scen", 0, 0, tiled=True)
    summed = jnp.sum(shares, axis=0) + jnp.pad(base, ((0, per_scen - share), (0, 0)))
    everyone = from_everyone(summed, "scen")

    hits = (
        jnp.arange(rows_dev, dtype=jnp.int32)[:, None] + my_row() * rows_dev == panel_vars[None, :]
    )
    rows_base = first_section + jnp.where(hits, barrier[:, None], 0.0)
    return pl.pallas_call(
        factor_kernel,
        out_shape=jax.ShapeDtypeStruct((rows_dev, win), F32),
        compiler_params=LIMIT,
    )(everyone, rows_base)


def solution(mesh):
    torus = Mesh(mesh.devices.reshape(mesh.shape["scen"], 4, 4, 2), ("scen", "zh", "zl", "xh"))
    return jax.shard_map(
        per_device,
        mesh=torus,
        in_specs=(
            P("scen", None, ROW),
            P("scen", ROW, None),
            P(ROW, None),
            P(ROW),
            P(),
            P(),
            P("scen"),
        ),
        out_specs=P(ROW, None),
        check_vma=False,
    )
```

```python
import jax
import jax.numpy as jnp
from jax import lax
from jax.experimental import pallas as pl
from jax.experimental.pallas import tpu as pltpu
from jax.sharding import Mesh
from jax.sharding import PartitionSpec as P

SLOTS = 31
GROUP = 8
PANEL = 128
ROW = ("z", "xh")
HIGHEST = lax.Precision.HIGHEST
F32 = jnp.float32
BF16 = jnp.bfloat16
LIMIT = pltpu.CompilerParams(vmem_limit_bytes=48 * 1024 * 1024)


def iota(shape, dim):
    return lax.broadcasted_iota(jnp.int32, shape, dim)


def contract(a, b, dim_a, dim_b, precision=None):
    return lax.dot_general(
        a, b, (((dim_a,), (dim_b,)), ((), ())), precision=precision, preferred_element_type=F32
    )


def swapped(x):
    return lax.ppermute(x, "xh", [(0, 1), (1, 0)])


def my_row():
    return lax.axis_index("z") * 2 + lax.axis_index("xh")


def places(panel_row, rows_pair, holders):
    win = panel_row.shape[1]
    holder = jnp.zeros_like(panel_row)
    for z in range(1, holders):
        holder = holder + (panel_row >= z * rows_pair).astype(jnp.int32)
    across = jnp.broadcast_to(holder, (win, win))
    earlier, later = iota((win, win), 0), iota((win, win), 1)
    down = jnp.sum(jnp.where(earlier == later, across, 0), axis=1, keepdims=True)
    same = (across == down) & (earlier < later)
    rank = jnp.sum(same.astype(jnp.int32), axis=0, keepdims=True)
    return holder, rank


def pick_kernel(
    turn_ref, panel_ref, border_ref, barrier_ref, first_ref, picked_ref, put_ref, rounds_ref
):
    rows_inv, rows_dev = border_ref.shape
    win = panel_ref.shape[1]
    z_count = put_ref.shape[0]
    panel_row = panel_ref[...]
    holder, rank = places(panel_row, 2 * rows_dev, z_count)
    rounds_ref[0] = jnp.max(rank) + 1
    place = rank - turn_ref[0] * SLOTS
    local = panel_row - my_row() * rows_dev
    in_slot = place == iota((SLOTS, win), 0)
    mine = in_slot & (local >= 0) & (local < rows_dev)
    source = jnp.sum(jnp.where(mine, local + 1, 0), axis=1, keepdims=True) - 1
    pick = (source == iota((SLOTS, rows_dev), 1)).astype(F32).astype(BF16)
    picked = contract(pick, border_ref[...], 1, 1)
    for z in range(z_count):
        put_ref[z] = jnp.where(in_slot & (holder == z), 1.0, 0.0).astype(BF16)
    share = win // lax.axis_size("scen")
    at = lax.axis_index("scen") * share + iota((share, win), 0)
    on_diagonal = at == iota((share, win), 1)
    own = jnp.sum(jnp.where(on_diagonal, local, 0), axis=1, keepdims=True)
    hit = own == iota((share, rows_dev), 1)
    base = contract(hit.astype(F32), first_ref[...], 1, 0, HIGHEST)
    term = jnp.sum(jnp.where(hit, barrier_ref[...], 0.0), axis=1, keepdims=True)
    base = base + jnp.where(on_diagonal, term, 0.0)
    rounded = base.astype(BF16).astype(F32)
    fold = rows_inv // win
    step = share // fold
    lanes = [
        jnp.concatenate([part[step * i : step * (i + 1)] for i in range(fold)], axis=1)
        for part in (rounded, base - rounded)
    ]
    picked_ref[...] = jnp.concatenate([*lanes, picked], axis=0).astype(BF16)


def gather_round(turn, panel_row, border, barrier_row, first_section):
    rows_inv, rows_dev = border.shape
    win = panel_row.shape[1]
    z_count = lax.axis_size("z")
    lines = SLOTS + 2 * win // lax.axis_size("scen") * win // rows_inv
    vmem = pl.BlockSpec(memory_space=pltpu.VMEM)
    smem = pl.BlockSpec(memory_space=pltpu.SMEM)
    picked, put, most = pl.pallas_call(
        pick_kernel,
        out_shape=(
            jax.ShapeDtypeStruct((lines, rows_inv), BF16),
            jax.ShapeDtypeStruct((z_count, SLOTS, win), BF16),
            jax.ShapeDtypeStruct((1,), jnp.int32),
        ),
        in_specs=[smem, vmem, vmem, vmem, vmem],
        out_specs=(vmem, vmem, smem),
        compiler_params=LIMIT,
    )(turn, panel_row, border, barrier_row, first_section)
    both = lax.all_gather(picked, "xh", axis=0)
    pair = both[0] + both[1]
    everyone = lax.all_gather(pair[-SLOTS:], "z", axis=0)
    columns = lax.dot_general(
        everyone, put, (((0, 1), (0, 1)), ((), ())), preferred_element_type=F32
    ).astype(BF16)
    return columns, most[0], pair[:-SLOTS]


def solve_kernel(own_ref, other_ref, columns_ref, extra_ref, out_ref):
    extra, rows_inv = extra_ref.shape
    win = columns_ref.shape[1]
    xh = lax.axis_index("xh")
    columns = columns_ref[...]
    own = contract(own_ref[...], columns, 1, 0)
    other = contract(other_ref[...], columns, 1, 0)
    low = jnp.where(xh == 0, own, other)
    high = jnp.where(xh == 0, other, own)
    parts = extra_ref[...].astype(F32)
    fold = rows_inv // win
    step = extra // 2
    lanes = [
        parts[step * p : step * (p + 1), win * i : win * (i + 1)] for p in range(2) for i in range(fold)
    ]
    out_ref[...] = jnp.concatenate([low, high, *lanes], axis=0).astype(BF16)


def term_kernel(columns_ref, border_ref, gathered_ref, prob_ref, slot_ref, out_ref, base_ref):
    z_count, lines, win = gathered_ref.shape
    rows_inv = border_ref.shape[0]
    scen_count, per_scen, _ = out_ref.shape
    share = win // scen_count
    step = rows_inv // z_count
    solved = gathered_ref[:, :step, :].reshape(rows_inv, win)
    match = iota(prob_ref.shape, 1) == slot_ref[...]
    weight = jnp.sum(jnp.where(match, prob_ref[...], 0.0), axis=1, keepdims=True)
    block = contract(columns_ref[...], solved, 0, 0) * weight
    out_ref[:, :share, :] = block.reshape(scen_count, share, win)
    term = contract(border_ref[...], solved, 0, 0) * weight
    out_ref[:, share:, :] = term.reshape(scen_count, per_scen - share, win)
    parts = jnp.sum(gathered_ref[:, step:, :].astype(F32), axis=0)
    base_ref[...] = parts[:share] + parts[share:]


def sum_kernel(shares_ref, base_ref, out_ref):
    share = base_ref.shape[0]
    total = jnp.sum(shares_ref[...], axis=0)
    total = jnp.concatenate([total[:share] + base_ref[...], total[share:]], axis=0)
    out_ref[...] = jnp.broadcast_to(total[None], out_ref.shape)


def inverse_factor(symmetric):
    size = symmetric.shape[0]
    count = size // GROUP
    work = [symmetric[GROUP * i : GROUP * (i + 1), :] for i in range(count)]
    lane, sub = iota((GROUP, size), 1), iota((GROUP, size), 0)
    result = []
    for group in range(count):
        low = group * GROUP
        block = work[group]
        inside = (lane >= low) & (lane < low + GROUP)
        lower = [[None] * GROUP for _ in range(GROUP)]
        scale = [None] * GROUP
        entry = [
            [jnp.broadcast_to(block[i : i + 1, low + j : low + j + 1], block.shape) for j in range(i + 1)]
            for i in range(GROUP)
        ]
        for j in range(GROUP):
            pivot = entry[j][j]
            for t in range(j):
                pivot = pivot - lower[j][t] * lower[j][t]
            scale[j] = lax.rsqrt(pivot)
            for i in range(j + 1, GROUP):
                value = entry[i][j]
                for t in range(j):
                    value = value - lower[i][t] * lower[j][t]
                lower[i][j] = value * scale[j]
        forward = []
        for i in range(GROUP):
            row = jnp.broadcast_to(block[i : i + 1, :], block.shape)
            row = jnp.where(inside, jnp.where(lane == low + i, 1.0, 0.0), row)
            for j in range(i):
                row = row - lower[i][j] * forward[j]
            forward.append(row * scale[i])
        done = forward[0]
        for i in range(1, GROUP):
            done = jnp.where(sub == i, forward[i], done)
        result.append(jnp.where(lane <= sub + low, done, 0.0))
        if group + 1 == count:
            break
        back = [None] * GROUP
        for i in reversed(range(GROUP)):
            row = forward[i]
            for j in range(i + 1, GROUP):
                row = row - lower[j][i] * back[j]
            back[i] = row * scale[i]
        for later in range(group + 1, count):
            old = work[later]
            new = jnp.where(inside, 0.0, old)
            for j in range(GROUP):
                new = new - old[:, low + j : low + j + 1] * back[j]
            work[later] = new
    return jnp.concatenate(result, axis=0)


def factor_kernel(gathered_ref, base_ref, out_ref):
    scen_count, per_scen, win = gathered_ref.shape
    share = win // scen_count
    diag = gathered_ref[:, :share, :].reshape(win, win)
    rows = gathered_ref[:, share:, :].reshape(base_ref.shape) + base_ref[...]

    def symmetric(i, j):
        one = diag[i : i + PANEL, j : j + PANEL]
        other = diag[j : j + PANEL, i : i + PANEL]
        return 0.5 * (one + other.T)

    first = inverse_factor(symmetric(0, 0))
    across = contract(symmetric(PANEL, 0), first, 1, 1, HIGHEST)
    second = inverse_factor(symmetric(PANEL, PANEL) - contract(across, across, 1, 1, HIGHEST))
    left = contract(rows[:, :PANEL], first, 1, 1, HIGHEST)
    right = rows[:, PANEL:] - contract(left, across, 1, 1, HIGHEST)
    out_ref[:, :PANEL] = left
    out_ref[:, PANEL:] = contract(right, second, 1, 1, HIGHEST)


def per_device(borders, kkt_inverse, first_section, barrier, panel_vars, probability, assignment):
    border, inverse_rows = borders[0], kkt_inverse[0]
    rows_inv, rows_dev = border.shape
    win = first_section.shape[1]
    scen_count = lax.axis_size("scen")
    share = win // scen_count
    panel_row, barrier_row = panel_vars[None, :], barrier[None, :]

    other_rows = swapped(inverse_rows)

    def turn(number):
        return gather_round(number[None], panel_row, border, barrier_row, first_section)

    columns, most, extra = turn(jnp.int32(0))
    _, columns = lax.while_loop(
        lambda state: state[0] * SLOTS < most,
        lambda state: (state[0] + 1, state[1] + turn(state[0])[0]),
        (jnp.int32(1), columns),
    )

    own_lines = 2 * inverse_rows.shape[0]
    message = pl.pallas_call(
        solve_kernel,
        out_shape=jax.ShapeDtypeStruct((own_lines + 2 * share, win), BF16),
        compiler_params=LIMIT,
    )(inverse_rows, other_rows, columns, extra)
    gathered = lax.all_gather(message, "z", axis=0)

    per_scen = share + rows_dev // scen_count
    terms, base = pl.pallas_call(
        term_kernel,
        out_shape=(
            jax.ShapeDtypeStruct((scen_count, per_scen, win), F32),
            jax.ShapeDtypeStruct((share, win), F32),
        ),
        compiler_params=LIMIT,
    )(columns, border, gathered, probability[None, :], assignment[None, :])
    shares = lax.all_to_all(terms, "scen", 0, 0, tiled=True)
    copies = pl.pallas_call(
        sum_kernel,
        out_shape=jax.ShapeDtypeStruct((scen_count, per_scen, win), F32),
        compiler_params=LIMIT,
    )(shares, base)
    everyone = lax.all_to_all(copies, "scen", 0, 0, tiled=True)

    hits = (
        jnp.arange(rows_dev, dtype=jnp.int32)[:, None] + my_row() * rows_dev == panel_vars[None, :]
    )
    rows_base = first_section + jnp.where(hits, barrier[:, None], 0.0)
    return pl.pallas_call(
        factor_kernel,
        out_shape=jax.ShapeDtypeStruct((rows_dev, win), F32),
        compiler_params=LIMIT,
    )(everyone, rows_base)


def solution(mesh):
    torus = Mesh(mesh.devices.reshape(mesh.shape["scen"], 16, 2), ("scen", "z", "xh"))
    return jax.shard_map(
        per_device,
        mesh=torus,
        in_specs=(
            P("scen", None, ROW),
            P("scen", ROW, None),
            P(ROW, None),
            P(ROW),
            P(),
            P(),
            P("scen"),
        ),
        out_specs=P(ROW, None),
        check_vma=False,
    )
```

```python
import jax
import jax.numpy as jnp
from jax import lax
from jax.experimental import pallas as pl
from jax.experimental.pallas import tpu as pltpu
from jax.sharding import Mesh
from jax.sharding import PartitionSpec as P

SLOTS = 31
GROUP = 8
PANEL = 128
ROW = ("z", "xh")
SCEN = ("chip", "core")
HIGHEST = lax.Precision.HIGHEST
F32 = jnp.float32
BF16 = jnp.bfloat16
LIMIT = pltpu.CompilerParams(vmem_limit_bytes=48 * 1024 * 1024)


def iota(shape, dim):
    return lax.broadcasted_iota(jnp.int32, shape, dim)


def contract(a, b, dim_a, dim_b, precision=None):
    return lax.dot_general(
        a, b, (((dim_a,), (dim_b,)), ((), ())), precision=precision, preferred_element_type=F32
    )


def swapped(x):
    return lax.ppermute(x, "xh", [(0, 1), (1, 0)])


def my_row():
    return lax.axis_index("z") * 2 + lax.axis_index("xh")


def places(panel_row, rows_pair, holders):
    win = panel_row.shape[1]
    holder = jnp.zeros_like(panel_row)
    for z in range(1, holders):
        holder = holder + (panel_row >= z * rows_pair).astype(jnp.int32)
    across = jnp.broadcast_to(holder, (win, win))
    earlier, later = iota((win, win), 0), iota((win, win), 1)
    down = jnp.sum(jnp.where(earlier == later, across, 0), axis=1, keepdims=True)
    same = (across == down) & (earlier < later)
    rank = jnp.sum(same.astype(jnp.int32), axis=0, keepdims=True)
    return holder, rank


def pick_kernel(
    turn_ref, panel_ref, border_ref, barrier_ref, first_ref, picked_ref, put_ref, rounds_ref
):
    rows_inv, rows_dev = border_ref.shape
    win = panel_ref.shape[1]
    z_count = put_ref.shape[0]
    panel_row = panel_ref[...]
    holder, rank = places(panel_row, 2 * rows_dev, z_count)
    rounds_ref[0] = jnp.max(rank) + 1
    place = rank - turn_ref[0] * SLOTS
    local = panel_row - my_row() * rows_dev
    in_slot = place == iota((SLOTS, win), 0)
    mine = in_slot & (local >= 0) & (local < rows_dev)
    source = jnp.sum(jnp.where(mine, local + 1, 0), axis=1, keepdims=True) - 1
    pick = (source == iota((SLOTS, rows_dev), 1)).astype(F32).astype(BF16)
    picked = contract(pick, border_ref[...], 1, 1)
    for z in range(z_count):
        put_ref[z] = jnp.where(in_slot & (holder == z), 1.0, 0.0).astype(BF16)
    share = win // lax.axis_size(SCEN)
    at = lax.axis_index(SCEN) * share + iota((share, win), 0)
    on_diagonal = at == iota((share, win), 1)
    own = jnp.sum(jnp.where(on_diagonal, local, 0), axis=1, keepdims=True)
    hit = own == iota((share, rows_dev), 1)
    base = contract(hit.astype(F32), first_ref[...], 1, 0, HIGHEST)
    term = jnp.sum(jnp.where(hit, barrier_ref[...], 0.0), axis=1, keepdims=True)
    base = base + jnp.where(on_diagonal, term, 0.0)
    rounded = base.astype(BF16).astype(F32)
    fold = rows_inv // win
    step = share // fold
    lanes = [
        jnp.concatenate([part[step * i : step * (i + 1)] for i in range(fold)], axis=1)
        for part in (rounded, base - rounded)
    ]
    picked_ref[...] = jnp.concatenate([*lanes, picked], axis=0).astype(BF16)


def gather_round(turn, panel_row, border, barrier_row, first_section):
    rows_inv, rows_dev = border.shape
    win = panel_row.shape[1]
    z_count = lax.axis_size("z")
    lines = SLOTS + 2 * win // lax.axis_size(SCEN) * win // rows_inv
    vmem = pl.BlockSpec(memory_space=pltpu.VMEM)
    smem = pl.BlockSpec(memory_space=pltpu.SMEM)
    picked, put, most = pl.pallas_call(
        pick_kernel,
        out_shape=(
            jax.ShapeDtypeStruct((lines, rows_inv), BF16),
            jax.ShapeDtypeStruct((z_count, SLOTS, win), BF16),
            jax.ShapeDtypeStruct((1,), jnp.int32),
        ),
        in_specs=[smem, vmem, vmem, vmem, vmem],
        out_specs=(vmem, vmem, smem),
        compiler_params=LIMIT,
    )(turn, panel_row, border, barrier_row, first_section)
    both = lax.all_gather(picked, "xh", axis=0)
    pair = both[0] + both[1]
    everyone = lax.all_gather(pair[-SLOTS:], "z", axis=0)
    columns = lax.dot_general(
        everyone, put, (((0, 1), (0, 1)), ((), ())), preferred_element_type=F32
    ).astype(BF16)
    return columns, most[0], pair[:-SLOTS]


def solve_kernel(own_ref, other_ref, columns_ref, extra_ref, out_ref):
    extra, rows_inv = extra_ref.shape
    win = columns_ref.shape[1]
    xh = lax.axis_index("xh")
    columns = columns_ref[...]
    own = contract(own_ref[...], columns, 1, 0)
    other = contract(other_ref[...], columns, 1, 0)
    low = jnp.where(xh == 0, own, other)
    high = jnp.where(xh == 0, other, own)
    parts = extra_ref[...].astype(F32)
    fold = rows_inv // win
    step = extra // 2
    lanes = [
        parts[step * p : step * (p + 1), win * i : win * (i + 1)] for p in range(2) for i in range(fold)
    ]
    out_ref[...] = jnp.concatenate([low, high, *lanes], axis=0).astype(BF16)


def term_kernel(
    columns_ref, border_ref, gathered_ref, prob_ref, slot_ref, keep_ref, give_ref, base_ref
):
    z_count, lines, win = gathered_ref.shape
    rows_inv = border_ref.shape[0]
    chips, per_scen, _ = keep_ref.shape
    share = base_ref.shape[0]
    step = rows_inv // z_count
    solved = gathered_ref[:, :step, :].reshape(rows_inv, win)
    weight = prob_ref[slot_ref[0]]
    core = lax.axis_index("core")
    block = contract(columns_ref[...], solved, 0, 0) * weight
    block = block.reshape(chips, 2, share, win)
    term = contract(border_ref[...], solved, 0, 0) * weight
    term = term.reshape(chips, 2, per_scen - share, win)
    keep_ref[:, :share, :] = jnp.where(core == 0, block[:, 0], block[:, 1])
    give_ref[:, :share, :] = jnp.where(core == 0, block[:, 1], block[:, 0])
    keep_ref[:, share:, :] = jnp.where(core == 0, term[:, 0], term[:, 1])
    give_ref[:, share:, :] = jnp.where(core == 0, term[:, 1], term[:, 0])
    parts = jnp.sum(gathered_ref[:, step:, :].astype(F32), axis=0)
    base_ref[...] = parts[:share] + parts[share:]


def pair_kernel(keep_ref, given_ref, out_ref):
    other = jnp.where(lax.axis_index("core") == 0, given_ref[1], given_ref[0])
    out_ref[...] = keep_ref[...] + other


def sum_kernel(shares_ref, base_ref, out_ref):
    share = base_ref.shape[0]
    total = jnp.sum(shares_ref[...], axis=0)
    total = jnp.concatenate([total[:share] + base_ref[...], total[share:]], axis=0)
    out_ref[...] = jnp.broadcast_to(total[None], out_ref.shape)


def tree_sum(terms):
    while len(terms) > 1:
        terms = [sum(terms[i : i + 2][1:], terms[i]) for i in range(0, len(terms), 2)]
    return terms[0]


def inverse_factor(symmetric):
    size = symmetric.shape[0]
    count = size // GROUP
    shape = (GROUP, size)
    work = [symmetric[GROUP * i : GROUP * (i + 1), :] for i in range(count)]
    lane, sub = iota(shape, 1), iota(shape, 0)
    result = []
    for group in range(count):
        low = group * GROUP
        block = work[group]
        inside = (lane >= low) & (lane < low + GROUP)
        entry = [
            [jnp.broadcast_to(block[i : i + 1, low + j : low + j + 1], shape) for j in range(i + 1)]
            for i in range(GROUP)
        ]
        pivot = [None] * GROUP
        lower = [[None] * GROUP for _ in range(GROUP)]
        for j in range(GROUP):
            pivot[j] = 1.0 / entry[j][j]
            for i in range(j + 1, GROUP):
                lower[i][j] = entry[i][j] * pivot[j]
            for i in range(j + 1, GROUP):
                for t in range(j + 1, i + 1):
                    entry[i][t] = entry[i][t] - (entry[i][j] * entry[t][j]) * pivot[j]
        unit = [[None] * GROUP for _ in range(GROUP)]
        for i in range(GROUP):
            for j in range(i):
                value = lower[i][j]
                for t in range(j + 1, i):
                    value = value + lower[i][t] * unit[t][j]
                unit[i][j] = -value
        rows = jnp.where(inside, jnp.where(lane == sub + low, 1.0, 0.0), block)
        terms = [rows]
        for j in range(GROUP - 1):
            column = jnp.zeros(shape, F32)
            for i in range(j + 1, GROUP):
                column = jnp.where(sub == i, unit[i][j], column)
            terms.append(column * jnp.broadcast_to(rows[j : j + 1, :], shape))
        forward = tree_sum(terms)
        scale = pivot[0]
        for i in range(1, GROUP):
            scale = jnp.where(sub == i, pivot[i], scale)
        result.append(jnp.where(lane <= sub + low, forward * jnp.sqrt(scale), 0.0))
        if group + 1 == count:
            break
        scaled = forward * scale
        scaled = [jnp.broadcast_to(scaled[i : i + 1, :], shape) for i in range(GROUP)]
        back = [
            tree_sum([scaled[j]] + [unit[i][j] * scaled[i] for i in range(j + 1, GROUP)])
            for j in range(GROUP)
        ]
        for later in range(group + 1, count):
            old = work[later]
            taken = tree_sum([old[:, low + j : low + j + 1] * back[j] for j in range(GROUP)])
            work[later] = jnp.where(inside, 0.0, old) - taken
    return jnp.concatenate(result, axis=0)


def factor_kernel(gathered_ref, base_ref, out_ref):
    cores, chips, per_scen, win = gathered_ref.shape
    share = win // (cores * chips)
    order = [(core, chip) for chip in range(chips) for core in range(cores)]
    diag = jnp.concatenate([gathered_ref[core, chip, :share, :] for core, chip in order], axis=0)
    rows = jnp.concatenate([gathered_ref[core, chip, share:, :] for core, chip in order], axis=0)
    rows = rows + base_ref[...]

    def symmetric(i, j):
        one = diag[i : i + PANEL, j : j + PANEL]
        other = diag[j : j + PANEL, i : i + PANEL]
        return 0.5 * (one + other.T)

    first = inverse_factor(symmetric(0, 0))
    across = contract(symmetric(PANEL, 0), first, 1, 1, HIGHEST)
    second = inverse_factor(symmetric(PANEL, PANEL) - contract(across, across, 1, 1, HIGHEST))
    left = contract(rows[:, :PANEL], first, 1, 1, HIGHEST)
    right = rows[:, PANEL:] - contract(left, across, 1, 1, HIGHEST)
    out_ref[:, :PANEL] = left
    out_ref[:, PANEL:] = contract(right, second, 1, 1, HIGHEST)


def per_device(borders, kkt_inverse, first_section, barrier, panel_vars, probability, assignment):
    border, inverse_rows = borders[0], kkt_inverse[0]
    rows_inv, rows_dev = border.shape
    win = first_section.shape[1]
    scen_count = lax.axis_size(SCEN)
    share = win // scen_count
    panel_row, barrier_row = panel_vars[None, :], barrier[None, :]

    other_rows = swapped(inverse_rows)

    def turn(number):
        return gather_round(number[None], panel_row, border, barrier_row, first_section)

    columns, most, extra = turn(jnp.int32(0))
    _, columns = lax.while_loop(
        lambda state: state[0] * SLOTS < most,
        lambda state: (state[0] + 1, state[1] + turn(state[0])[0]),
        (jnp.int32(1), columns),
    )

    own_lines = 2 * inverse_rows.shape[0]
    message = pl.pallas_call(
        solve_kernel,
        out_shape=jax.ShapeDtypeStruct((own_lines + 2 * share, win), BF16),
        compiler_params=LIMIT,
    )(inverse_rows, other_rows, columns, extra)
    gathered = lax.all_gather(message, "z", axis=0)

    per_scen = share + rows_dev // scen_count
    vmem = pl.BlockSpec(memory_space=pltpu.VMEM)
    smem = pl.BlockSpec(memory_space=pltpu.SMEM)
    half = jax.ShapeDtypeStruct((lax.axis_size("chip"), per_scen, win), F32)
    keep, give, base = pl.pallas_call(
        term_kernel,
        out_shape=(half, half, jax.ShapeDtypeStruct((share, win), F32)),
        in_specs=[vmem, vmem, vmem, smem, smem],
        compiler_params=LIMIT,
    )(columns, border, gathered, probability, assignment)
    given = lax.all_gather(give, "core", axis=0)
    pair = pl.pallas_call(pair_kernel, out_shape=half, compiler_params=LIMIT)(keep, given)
    shares = lax.all_to_all(pair, "chip", 0, 0, tiled=True)
    copies = pl.pallas_call(sum_kernel, out_shape=half, compiler_params=LIMIT)(shares, base)
    everyone = lax.all_to_all(copies, "chip", 0, 0, tiled=True)
    everyone = lax.all_gather(everyone, "core", axis=0)

    hits = (
        jnp.arange(rows_dev, dtype=jnp.int32)[:, None] + my_row() * rows_dev == panel_vars[None, :]
    )
    rows_base = first_section + jnp.where(hits, barrier[:, None], 0.0)
    return pl.pallas_call(
        factor_kernel,
        out_shape=jax.ShapeDtypeStruct((rows_dev, win), F32),
        compiler_params=LIMIT,
    )(everyone, rows_base)


def solution(mesh):
    torus = Mesh(mesh.devices.reshape(8, 2, 16, 2), (*SCEN, *ROW))
    return jax.shard_map(
        per_device,
        mesh=torus,
        in_specs=(
            P(SCEN, None, ROW),
            P(SCEN, ROW, None),
            P(ROW, None),
            P(ROW),
            P(),
            P(),
            P(SCEN),
        ),
        out_specs=P(ROW, None),
        check_vma=False,
    )
```

```python
import jax
import jax.numpy as jnp
from jax import lax
from jax.experimental import pallas as pl
from jax.experimental.pallas import tpu as pltpu
from jax.sharding import Mesh
from jax.sharding import PartitionSpec as P

SLOTS = 31
GROUP = 8
PANEL = 128
ROW = ("z", "xh")
SCEN = ("chip", "core")
HIGHEST = lax.Precision.HIGHEST
F32 = jnp.float32
BF16 = jnp.bfloat16
LIMIT = pltpu.CompilerParams(vmem_limit_bytes=48 * 1024 * 1024)


def iota(shape, dim):
    return lax.broadcasted_iota(jnp.int32, shape, dim)


def contract(a, b, dim_a, dim_b, precision=None):
    return lax.dot_general(
        a, b, (((dim_a,), (dim_b,)), ((), ())), precision=precision, preferred_element_type=F32
    )


def my_row():
    return lax.axis_index("z") * 2 + lax.axis_index("xh")


def places(panel_row, rows_pair, holders):
    win = panel_row.shape[1]
    holder = jnp.zeros_like(panel_row)
    for z in range(1, holders):
        holder = holder + (panel_row >= z * rows_pair).astype(jnp.int32)
    across = jnp.broadcast_to(holder, (win, win))
    earlier, later = iota((win, win), 0), iota((win, win), 1)
    down = jnp.sum(jnp.where(earlier == later, across, 0), axis=1, keepdims=True)
    same = (across == down) & (earlier < later)
    rank = jnp.sum(same.astype(jnp.int32), axis=0, keepdims=True)
    return holder, rank


def pick_kernel(
    turn_ref,
    prob_ref,
    slot_ref,
    panel_ref,
    border_ref,
    inverse_ref,
    barrier_ref,
    first_ref,
    message_ref,
    put_ref,
    weight_ref,
    rounds_ref,
):
    rows_inv, rows_dev = border_ref.shape
    win = first_ref.shape[1]
    z_count = put_ref.shape[0]
    weight_ref[...] = jnp.full(weight_ref.shape, prob_ref[slot_ref[0]], F32)
    panel_row = panel_ref[...][None, :]
    holder, rank = places(panel_row, 2 * rows_dev, z_count)
    rounds_ref[0] = jnp.max(rank) + 1
    place = rank - turn_ref[0] * SLOTS
    local = panel_row - my_row() * rows_dev
    in_slot = place == iota((SLOTS, win), 0)
    mine = in_slot & (local >= 0) & (local < rows_dev)
    source = jnp.sum(jnp.where(mine, local + 1, 0), axis=1, keepdims=True) - 1
    pick = (source == iota((SLOTS, rows_dev), 1)).astype(F32).astype(BF16)
    picked = contract(pick, border_ref[...], 1, 1)
    for z in range(z_count):
        put_ref[z] = jnp.where(in_slot & (holder == z), 1.0, 0.0).astype(BF16)
    share = win // lax.axis_size(SCEN)
    at = lax.axis_index(SCEN) * share + iota((share, win), 0)
    on_diagonal = at == iota((share, win), 1)
    own = jnp.sum(jnp.where(on_diagonal, local, 0), axis=1, keepdims=True)
    hit = own == iota((share, rows_dev), 1)
    base = contract(hit.astype(F32), first_ref[...], 1, 0, HIGHEST)
    term = jnp.sum(jnp.where(hit, barrier_ref[...][None, :], 0.0), axis=1, keepdims=True)
    base = base + jnp.where(on_diagonal, term, 0.0)
    rounded = base.astype(BF16).astype(F32)
    fold = rows_inv // win
    step = share // fold
    lanes = [
        jnp.concatenate([part[step * i : step * (i + 1)] for i in range(fold)], axis=1)
        for part in (rounded, base - rounded)
    ]
    lines = [*lanes, inverse_ref[...].astype(F32), picked]
    message_ref[...] = jnp.concatenate(lines, axis=0).astype(BF16)


def gather_round(turn, border, inverse_rows, first_section, barrier, panel_vars, prob, slot):
    rows_inv, rows_dev = border.shape
    win = panel_vars.shape[0]
    z_count = lax.axis_size("z")
    extra = 2 * win // lax.axis_size(SCEN) * win // rows_inv
    vmem = pl.BlockSpec(memory_space=pltpu.VMEM)
    smem = pl.BlockSpec(memory_space=pltpu.SMEM)
    message, put, weight, most = pl.pallas_call(
        pick_kernel,
        out_shape=(
            jax.ShapeDtypeStruct((extra + inverse_rows.shape[0] + SLOTS, rows_inv), BF16),
            jax.ShapeDtypeStruct((z_count, SLOTS, win), BF16),
            jax.ShapeDtypeStruct((1, win), F32),
            jax.ShapeDtypeStruct((1,), jnp.int32),
        ),
        in_specs=[smem, smem, smem, vmem, vmem, vmem, vmem, vmem],
        out_specs=(vmem, vmem, vmem, smem),
        compiler_params=LIMIT,
    )(turn, prob, slot, panel_vars, border, inverse_rows, barrier, first_section)
    both = lax.all_gather(message, "xh", axis=0)
    mine = both[0, -SLOTS:] + both[1, -SLOTS:]
    everyone = lax.all_gather(mine, "z", axis=0)
    columns = lax.dot_general(
        everyone, put, (((0, 1), (0, 1)), ((), ())), preferred_element_type=F32
    ).astype(BF16)
    return columns, most[0], both[:, :-SLOTS], weight


def solve_kernel(both_ref, columns_ref, out_ref):
    _, lines, rows_inv = both_ref.shape
    win = columns_ref.shape[1]
    own = rows_inv // (2 * lax.axis_size("z"))
    extra = lines - own
    both = both_ref[...].astype(F32)
    rows = both[:, extra:, :].reshape(2 * own, rows_inv).astype(BF16)
    solved = contract(rows, columns_ref[...], 1, 0)
    parts = both[0, :extra, :] + both[1, :extra, :]
    fold = rows_inv // win
    step = extra // 2
    lanes = [
        parts[step * p : step * (p + 1), win * i : win * (i + 1)] for p in range(2) for i in range(fold)
    ]
    out_ref[...] = jnp.concatenate([solved, *lanes], axis=0).astype(BF16)


def term_kernel(columns_ref, border_ref, gathered_ref, weight_ref, keep_ref, give_ref, base_ref):
    z_count, lines, win = gathered_ref.shape
    rows_inv = border_ref.shape[0]
    chips, per_scen, _ = keep_ref.shape
    share = base_ref.shape[0]
    step = rows_inv // z_count
    solved = gathered_ref[:, :step, :].reshape(rows_inv, win)
    weight = weight_ref[...]
    block = contract(columns_ref[...], solved, 0, 0) * weight
    block = block.reshape(chips, 2, share, win)
    term = contract(border_ref[...], solved, 0, 0) * weight
    term = term.reshape(chips, 2, per_scen - share, win)
    for core in range(2):

        @pl.when(lax.axis_index("core") == core)
        def _(core=core):
            keep_ref[:, :share, :] = block[:, core]
            keep_ref[:, share:, :] = term[:, core]
            give_ref[:, :share, :] = block[:, 1 - core]
            give_ref[:, share:, :] = term[:, 1 - core]

    parts = jnp.sum(gathered_ref[:, step:, :].astype(F32), axis=0)
    base_ref[...] = parts[:share] + parts[share:]


def pair_kernel(keep_ref, given_ref, out_ref):
    out_ref[...] = keep_ref[...] + given_ref[1 - lax.axis_index("core")]


def sum_kernel(shares_ref, base_ref, out_ref):
    share = base_ref.shape[0]
    total = jnp.sum(shares_ref[...], axis=0)
    total = jnp.concatenate([total[:share] + base_ref[...], total[share:]], axis=0)
    out_ref[...] = jnp.broadcast_to(total[None], out_ref.shape)


def tree_sum(terms):
    while len(terms) > 1:
        terms = [sum(terms[i : i + 2][1:], terms[i]) for i in range(0, len(terms), 2)]
    return terms[0]


def inverse_factor(symmetric):
    size = symmetric.shape[0]
    count = size // GROUP
    shape = (GROUP, size)
    work = [symmetric[GROUP * i : GROUP * (i + 1), :] for i in range(count)]
    lane, sub = iota(shape, 1), iota(shape, 0)
    result = []
    for group in range(count):
        low = group * GROUP
        block = work[group]
        inside = (lane >= low) & (lane < low + GROUP)
        entry = [
            [jnp.broadcast_to(block[i : i + 1, low + j : low + j + 1], shape) for j in range(i + 1)]
            for i in range(GROUP)
        ]
        pivot = [None] * GROUP
        lower = [[None] * GROUP for _ in range(GROUP)]
        for j in range(GROUP):
            pivot[j] = 1.0 / entry[j][j]
            for i in range(j + 1, GROUP):
                lower[i][j] = entry[i][j] * pivot[j]
            for i in range(j + 1, GROUP):
                for t in range(j + 1, i + 1):
                    entry[i][t] = entry[i][t] - (entry[i][j] * entry[t][j]) * pivot[j]
        unit = [[None] * GROUP for _ in range(GROUP)]
        for i in range(GROUP):
            for j in range(i):
                value = lower[i][j]
                for t in range(j + 1, i):
                    value = value + lower[i][t] * unit[t][j]
                unit[i][j] = -value
        rows = jnp.where(inside, jnp.where(lane == sub + low, 1.0, 0.0), block)
        terms = [rows]
        for j in range(GROUP - 1):
            column = jnp.zeros(shape, F32)
            for i in range(j + 1, GROUP):
                column = jnp.where(sub == i, unit[i][j], column)
            terms.append(column * jnp.broadcast_to(rows[j : j + 1, :], shape))
        forward = tree_sum(terms)
        scale = pivot[0]
        for i in range(1, GROUP):
            scale = jnp.where(sub == i, pivot[i], scale)
        result.append(jnp.where(lane <= sub + low, forward * jnp.sqrt(scale), 0.0))
        if group + 1 == count:
            break
        scaled = forward * scale
        scaled = [jnp.broadcast_to(scaled[i : i + 1, :], shape) for i in range(GROUP)]
        back = [
            tree_sum([scaled[j]] + [unit[i][j] * scaled[i] for i in range(j + 1, GROUP)])
            for j in range(GROUP)
        ]
        for later in range(group + 1, count):
            old = work[later]
            taken = tree_sum([old[:, low + j : low + j + 1] * back[j] for j in range(GROUP)])
            work[later] = jnp.where(inside, 0.0, old) - taken
    return jnp.concatenate(result, axis=0)


def factor_kernel(gathered_ref, base_ref, out_ref):
    cores, chips, per_scen, win = gathered_ref.shape
    share = win // (cores * chips)
    order = [(core, chip) for chip in range(chips) for core in range(cores)]
    diag = jnp.concatenate([gathered_ref[core, chip, :share, :] for core, chip in order], axis=0)
    rows = jnp.concatenate([gathered_ref[core, chip, share:, :] for core, chip in order], axis=0)
    rows = rows + base_ref[...]

    def symmetric(i, j):
        one = diag[i : i + PANEL, j : j + PANEL]
        other = diag[j : j + PANEL, i : i + PANEL]
        return 0.5 * (one + other.T)

    first = inverse_factor(symmetric(0, 0))
    across = contract(symmetric(PANEL, 0), first, 1, 1, HIGHEST)
    second = inverse_factor(symmetric(PANEL, PANEL) - contract(across, across, 1, 1, HIGHEST))
    left = contract(rows[:, :PANEL], first, 1, 1, HIGHEST)
    right = rows[:, PANEL:] - contract(left, across, 1, 1, HIGHEST)
    out_ref[:, :PANEL] = left
    out_ref[:, PANEL:] = contract(right, second, 1, 1, HIGHEST)


def per_device(borders, kkt_inverse, first_section, barrier, panel_vars, probability, assignment):
    border, inverse_rows = borders[0], kkt_inverse[0]
    rows_inv, rows_dev = border.shape
    win = first_section.shape[1]
    scen_count = lax.axis_size(SCEN)
    share = win // scen_count

    def turn(number):
        return gather_round(
            number[None],
            border,
            inverse_rows,
            first_section,
            barrier,
            panel_vars,
            probability,
            assignment,
        )

    columns, most, both, weight = turn(jnp.int32(0))
    _, columns = lax.while_loop(
        lambda state: state[0] * SLOTS < most,
        lambda state: (state[0] + 1, state[1] + turn(state[0])[0]),
        (jnp.int32(1), columns),
    )

    own_lines = 2 * inverse_rows.shape[0]
    message = pl.pallas_call(
        solve_kernel,
        out_shape=jax.ShapeDtypeStruct((own_lines + 2 * share, win), BF16),
        compiler_params=LIMIT,
    )(both, columns)
    gathered = lax.all_gather(message, "z", axis=0)

    per_scen = share + rows_dev // scen_count
    half = jax.ShapeDtypeStruct((lax.axis_size("chip"), per_scen, win), F32)
    keep, give, base = pl.pallas_call(
        term_kernel,
        out_shape=(half, half, jax.ShapeDtypeStruct((share, win), F32)),
        compiler_params=LIMIT,
    )(columns, border, gathered, weight)
    given = lax.all_gather(give, "core", axis=0)
    pair = pl.pallas_call(pair_kernel, out_shape=half, compiler_params=LIMIT)(keep, given)
    shares = lax.all_to_all(pair, "chip", 0, 0, tiled=True)
    copies = pl.pallas_call(sum_kernel, out_shape=half, compiler_params=LIMIT)(shares, base)
    everyone = lax.all_to_all(copies, "chip", 0, 0, tiled=True)
    everyone = lax.all_gather(everyone, "core", axis=0)

    hits = (
        jnp.arange(rows_dev, dtype=jnp.int32)[:, None] + my_row() * rows_dev == panel_vars[None, :]
    )
    rows_base = first_section + jnp.where(hits, barrier[:, None], 0.0)
    return pl.pallas_call(
        factor_kernel,
        out_shape=jax.ShapeDtypeStruct((rows_dev, win), F32),
        compiler_params=LIMIT,
    )(everyone, rows_base)


def solution(mesh):
    torus = Mesh(mesh.devices.reshape(8, 2, 16, 2), (*SCEN, *ROW))
    return jax.shard_map(
        per_device,
        mesh=torus,
        in_specs=(
            P(SCEN, None, ROW),
            P(SCEN, ROW, None),
            P(ROW, None),
            P(ROW),
            P(),
            P(),
            P(SCEN),
        ),
        out_specs=P(ROW, None),
        check_vma=False,
    )
```

```python
import jax
import jax.numpy as jnp
from jax import lax
from jax.experimental import pallas as pl
from jax.experimental.pallas import tpu as pltpu
from jax.sharding import Mesh
from jax.sharding import PartitionSpec as P

SLOTS = 31
GROUP = 8
PANEL = 128
ROW = ("z", "xh")
SCEN = ("chip", "core")
HIGHEST = lax.Precision.HIGHEST
F32 = jnp.float32
BF16 = jnp.bfloat16
LIMIT = pltpu.CompilerParams(vmem_limit_bytes=48 * 1024 * 1024)


def iota(shape, dim):
    return lax.broadcasted_iota(jnp.int32, shape, dim)


def contract(a, b, dim_a, dim_b, precision=None):
    return lax.dot_general(
        a, b, (((dim_a,), (dim_b,)), ((), ())), precision=precision, preferred_element_type=F32
    )


def my_row():
    return lax.axis_index("z") * 2 + lax.axis_index("xh")


def places(panel_row, rows_pair, holders):
    win = panel_row.shape[1]
    holder = jnp.zeros_like(panel_row)
    for z in range(1, holders):
        holder = holder + (panel_row >= z * rows_pair).astype(jnp.int32)
    across = jnp.broadcast_to(holder, (win, win))
    earlier, later = iota((win, win), 0), iota((win, win), 1)
    down = jnp.sum(jnp.where(earlier == later, across, 0), axis=1, keepdims=True)
    same = (across == down) & (earlier < later)
    rank = jnp.sum(same.astype(jnp.int32), axis=0, keepdims=True)
    return holder, rank


def pick_kernel(
    turn_ref,
    prob_ref,
    slot_ref,
    panel_ref,
    border_ref,
    inverse_ref,
    barrier_ref,
    first_ref,
    message_ref,
    put_ref,
    weight_ref,
    rounds_ref,
):
    rows_inv, rows_dev = border_ref.shape
    win = first_ref.shape[1]
    z_count = put_ref.shape[0]
    weight_ref[...] = jnp.full(weight_ref.shape, prob_ref[slot_ref[0]], F32)
    panel_row = panel_ref[...][None, :]
    holder, rank = places(panel_row, 2 * rows_dev, z_count)
    rounds_ref[0] = jnp.max(rank) + 1
    place = rank - turn_ref[0] * SLOTS
    local = panel_row - my_row() * rows_dev
    in_slot = place == iota((SLOTS, win), 0)
    mine = in_slot & (local >= 0) & (local < rows_dev)
    source = jnp.sum(jnp.where(mine, local + 1, 0), axis=1, keepdims=True) - 1
    pick = (source == iota((SLOTS, rows_dev), 1)).astype(F32).astype(BF16)
    picked = contract(pick, border_ref[...], 1, 1)
    for z in range(z_count):
        put_ref[z] = jnp.where(in_slot & (holder == z), 1.0, 0.0).astype(BF16)
    share = win // lax.axis_size(SCEN)
    at = lax.axis_index(SCEN) * share + iota((share, win), 0)
    on_diagonal = at == iota((share, win), 1)
    own = jnp.sum(jnp.where(on_diagonal, local, 0), axis=1, keepdims=True)
    hit = own == iota((share, rows_dev), 1)
    base = contract(hit.astype(F32), first_ref[...], 1, 0, HIGHEST)
    term = jnp.sum(jnp.where(hit, barrier_ref[...][None, :], 0.0), axis=1, keepdims=True)
    base = base + jnp.where(on_diagonal, term, 0.0)
    rounded = base.astype(BF16).astype(F32)
    fold = rows_inv // win
    step = share // fold
    lanes = [
        jnp.concatenate([part[step * i : step * (i + 1)] for i in range(fold)], axis=1)
        for part in (rounded, base - rounded)
    ]
    lines = [*lanes, inverse_ref[...].astype(F32), picked]
    message_ref[...] = jnp.concatenate(lines, axis=0).astype(BF16)


def gather_round(turn, border, inverse_rows, first_section, barrier, panel_vars, prob, slot):
    rows_inv, rows_dev = border.shape
    win = panel_vars.shape[0]
    z_count = lax.axis_size("z")
    extra = 2 * win // lax.axis_size(SCEN) * win // rows_inv
    vmem = pl.BlockSpec(memory_space=pltpu.VMEM)
    smem = pl.BlockSpec(memory_space=pltpu.SMEM)
    message, put, weight, most = pl.pallas_call(
        pick_kernel,
        out_shape=(
            jax.ShapeDtypeStruct((extra + inverse_rows.shape[0] + SLOTS, rows_inv), BF16),
            jax.ShapeDtypeStruct((z_count, SLOTS, win), BF16),
            jax.ShapeDtypeStruct((1, win), F32),
            jax.ShapeDtypeStruct((1,), jnp.int32),
        ),
        in_specs=[smem, smem, smem, vmem, vmem, vmem, vmem, vmem],
        out_specs=(vmem, vmem, vmem, smem),
        compiler_params=LIMIT,
    )(turn, prob, slot, panel_vars, border, inverse_rows, barrier, first_section)
    both = lax.all_gather(message, "xh", axis=0)
    mine = both[0, -SLOTS:] + both[1, -SLOTS:]
    everyone = lax.all_gather(mine, "z", axis=0)
    columns = lax.dot_general(
        everyone, put, (((0, 1), (0, 1)), ((), ())), preferred_element_type=F32
    ).astype(BF16)
    return columns, most[0], both[:, :-SLOTS], weight


def solve_kernel(both_ref, columns_ref, out_ref):
    _, lines, rows_inv = both_ref.shape
    win = columns_ref.shape[1]
    own = rows_inv // (2 * lax.axis_size("z"))
    extra = lines - own
    both = both_ref[...].astype(F32)
    rows = both[:, extra:, :].reshape(2 * own, rows_inv).astype(BF16)
    solved = contract(rows, columns_ref[...], 1, 0)
    parts = both[0, :extra, :] + both[1, :extra, :]
    fold = rows_inv // win
    step = extra // 2
    lanes = [
        parts[step * p : step * (p + 1), win * i : win * (i + 1)] for p in range(2) for i in range(fold)
    ]
    out_ref[...] = jnp.concatenate([solved, *lanes], axis=0).astype(BF16)


def term_kernel(columns_ref, border_ref, gathered_ref, weight_ref, keep_ref, give_ref, base_ref):
    z_count, lines, win = gathered_ref.shape
    rows_inv = border_ref.shape[0]
    chips, per_scen, _ = keep_ref.shape
    share = base_ref.shape[0]
    step = rows_inv // z_count
    solved = gathered_ref[:, :step, :].reshape(rows_inv, win)
    weight = weight_ref[...]
    block = contract(columns_ref[...], solved, 0, 0) * weight
    block = block.reshape(chips, 2, share, win)
    term = contract(border_ref[...], solved, 0, 0) * weight
    term = term.reshape(chips, 2, per_scen - share, win)
    for core in range(2):

        @pl.when(lax.axis_index("core") == core)
        def _(core=core):
            keep_ref[:, :share, :] = block[:, core]
            keep_ref[:, share:, :] = term[:, core]
            give_ref[:, :share, :] = block[:, 1 - core]
            give_ref[:, share:, :] = term[:, 1 - core]

    parts = jnp.sum(gathered_ref[:, step:, :].astype(F32), axis=0)
    base_ref[...] = parts[:share] + parts[share:]


def tree_sum(terms):
    while len(terms) > 1:
        terms = [sum(terms[i : i + 2][1:], terms[i]) for i in range(0, len(terms), 2)]
    return terms[0]


def inverse_factor(symmetric):
    size = symmetric.shape[0]
    count = size // GROUP
    shape = (GROUP, size)
    work = [symmetric[GROUP * i : GROUP * (i + 1), :] for i in range(count)]
    lane, sub = iota(shape, 1), iota(shape, 0)
    result = []
    for group in range(count):
        low = group * GROUP
        block = work[group]
        inside = (lane >= low) & (lane < low + GROUP)
        entry = [
            [jnp.broadcast_to(block[i : i + 1, low + j : low + j + 1], shape) for j in range(i + 1)]
            for i in range(GROUP)
        ]
        pivot = [None] * GROUP
        lower = [[None] * GROUP for _ in range(GROUP)]
        for j in range(GROUP):
            pivot[j] = 1.0 / entry[j][j]
            for i in range(j + 1, GROUP):
                lower[i][j] = entry[i][j] * pivot[j]
            for i in range(j + 1, GROUP):
                for t in range(j + 1, i + 1):
                    entry[i][t] = entry[i][t] - (entry[i][j] * entry[t][j]) * pivot[j]
        unit = [[None] * GROUP for _ in range(GROUP)]
        for i in range(GROUP):
            for j in range(i):
                value = lower[i][j]
                for t in range(j + 1, i):
                    value = value + lower[i][t] * unit[t][j]
                unit[i][j] = -value
        rows = jnp.where(inside, jnp.where(lane == sub + low, 1.0, 0.0), block)
        terms = [rows]
        for j in range(GROUP - 1):
            column = jnp.zeros(shape, F32)
            for i in range(j + 1, GROUP):
                column = jnp.where(sub == i, unit[i][j], column)
            terms.append(column * jnp.broadcast_to(rows[j : j + 1, :], shape))
        forward = tree_sum(terms)
        scale = pivot[0]
        for i in range(1, GROUP):
            scale = jnp.where(sub == i, pivot[i], scale)
        result.append(jnp.where(lane <= sub + low, forward * jnp.sqrt(scale), 0.0))
        if group + 1 == count:
            break
        scaled = forward * scale
        scaled = [jnp.broadcast_to(scaled[i : i + 1, :], shape) for i in range(GROUP)]
        back = [
            tree_sum([scaled[j]] + [unit[i][j] * scaled[i] for i in range(j + 1, GROUP)])
            for j in range(GROUP)
        ]
        near = group + 2 if count - group > 4 else count
        for later in range(group + 1, near):
            old = work[later]
            taken = tree_sum([old[:, low + j : low + j + 1] * back[j] for j in range(GROUP)])
            work[later] = jnp.where(inside, 0.0, old) - taken
        if near < count:
            stacked = back[0]
            for j in range(1, GROUP):
                stacked = jnp.where(sub == j, back[j], stacked)
            zero = jnp.zeros(shape, F32)
            spread = [stacked if i == group else zero for i in range(count)]
            taken = contract(
                jnp.concatenate(work[near:], axis=0), jnp.concatenate(spread, axis=0), 1, 0, HIGHEST
            )
            for later in range(near, count):
                at = GROUP * (later - near)
                work[later] = jnp.where(inside, 0.0, work[later]) - taken[at : at + GROUP]
    return jnp.concatenate(result, axis=0)


def factor_kernel(gathered_ref, base_ref, out_ref):
    cores, chips, per_scen, win = gathered_ref.shape
    share = win // (cores * chips)
    order = [(core, chip) for chip in range(chips) for core in range(cores)]
    diag = jnp.concatenate([gathered_ref[core, chip, :share, :] for core, chip in order], axis=0)
    rows = jnp.concatenate([gathered_ref[core, chip, share:, :] for core, chip in order], axis=0)
    rows = rows + base_ref[...]

    def symmetric(i, j):
        one = diag[i : i + PANEL, j : j + PANEL]
        other = diag[j : j + PANEL, i : i + PANEL]
        return 0.5 * (one + other.T)

    first = inverse_factor(symmetric(0, 0))
    across = contract(symmetric(PANEL, 0), first, 1, 1, HIGHEST)
    second = inverse_factor(symmetric(PANEL, PANEL) - contract(across, across, 1, 1, HIGHEST))
    left = contract(rows[:, :PANEL], first, 1, 1, HIGHEST)
    right = rows[:, PANEL:] - contract(left, across, 1, 1, HIGHEST)
    out_ref[:, :PANEL] = left
    out_ref[:, PANEL:] = contract(right, second, 1, 1, HIGHEST)


def per_device(borders, kkt_inverse, first_section, barrier, panel_vars, probability, assignment):
    border, inverse_rows = borders[0], kkt_inverse[0]
    rows_inv, rows_dev = border.shape
    win = first_section.shape[1]
    scen_count = lax.axis_size(SCEN)
    share = win // scen_count

    def turn(number):
        return gather_round(
            number[None],
            border,
            inverse_rows,
            first_section,
            barrier,
            panel_vars,
            probability,
            assignment,
        )

    columns, most, both, weight = turn(jnp.int32(0))
    _, columns = lax.while_loop(
        lambda state: state[0] * SLOTS < most,
        lambda state: (state[0] + 1, state[1] + turn(state[0])[0]),
        (jnp.int32(1), columns),
    )

    own_lines = 2 * inverse_rows.shape[0]
    message = pl.pallas_call(
        solve_kernel,
        out_shape=jax.ShapeDtypeStruct((own_lines + 2 * share, win), BF16),
        compiler_params=LIMIT,
    )(both, columns)
    gathered = lax.all_gather(message, "z", axis=0)

    per_scen = share + rows_dev // scen_count
    half = jax.ShapeDtypeStruct((lax.axis_size("chip"), per_scen, win), F32)
    keep, give, base = pl.pallas_call(
        term_kernel,
        out_shape=(half, half, jax.ShapeDtypeStruct((share, win), F32)),
        compiler_params=LIMIT,
    )(columns, border, gathered, weight)
    given = lax.all_gather(give, "core", axis=0)
    pair = keep + lax.dynamic_index_in_dim(given, 1 - lax.axis_index("core"), 0, keepdims=False)
    shares = lax.all_to_all(pair, "chip", 0, 0, tiled=True)
    total = jnp.sum(shares, axis=0) + jnp.pad(base, ((0, per_scen - share), (0, 0)))
    copies = jnp.broadcast_to(total[None], half.shape)
    everyone = lax.all_to_all(copies, "chip", 0, 0, tiled=True)
    everyone = lax.all_gather(everyone, "core", axis=0)

    hits = (
        jnp.arange(rows_dev, dtype=jnp.int32)[:, None] + my_row() * rows_dev == panel_vars[None, :]
    )
    rows_base = first_section + jnp.where(hits, barrier[:, None], 0.0)
    return pl.pallas_call(
        factor_kernel,
        out_shape=jax.ShapeDtypeStruct((rows_dev, win), F32),
        compiler_params=LIMIT,
    )(everyone, rows_base)


def solution(mesh):
    torus = Mesh(mesh.devices.reshape(8, 2, 16, 2), (*SCEN, *ROW))
    return jax.shard_map(
        per_device,
        mesh=torus,
        in_specs=(
            P(SCEN, None, ROW),
            P(SCEN, ROW, None),
            P(ROW, None),
            P(ROW),
            P(),
            P(),
            P(SCEN),
        ),
        out_specs=P(ROW, None),
        check_vma=False,
    )
```

```python
import jax
import jax.numpy as jnp
from jax import lax
from jax.experimental import pallas as pl
from jax.experimental.pallas import tpu as pltpu
from jax.sharding import Mesh
from jax.sharding import PartitionSpec as P

SLOTS = 31
GROUP = 8
PANEL = 128
ROW = ("z", "xh")
SCEN = ("chip", "core")
HIGHEST = lax.Precision.HIGHEST
F32 = jnp.float32
BF16 = jnp.bfloat16
LIMIT = pltpu.CompilerParams(vmem_limit_bytes=48 * 1024 * 1024)


def iota(shape, dim):
    return lax.broadcasted_iota(jnp.int32, shape, dim)


def contract(a, b, dim_a, dim_b, precision=None):
    return lax.dot_general(
        a, b, (((dim_a,), (dim_b,)), ((), ())), precision=precision, preferred_element_type=F32
    )


def contract_split(a, b, dim_a, dim_b):
    a_high, b_high = a.astype(BF16), b.astype(BF16)
    a_low = (a - a_high.astype(F32)).astype(BF16)
    b_low = (b - b_high.astype(F32)).astype(BF16)
    small = contract(a_high, b_low, dim_a, dim_b) + contract(a_low, b_high, dim_a, dim_b)
    return contract(a_high, b_high, dim_a, dim_b) + small


def my_row():
    return lax.axis_index("z") * 2 + lax.axis_index("xh")


def places(panel_row, rows_pair, holders):
    win = panel_row.shape[1]
    holder = jnp.zeros_like(panel_row)
    for z in range(1, holders):
        holder = holder + (panel_row >= z * rows_pair).astype(jnp.int32)
    across = jnp.broadcast_to(holder, (win, win))
    earlier, later = iota((win, win), 0), iota((win, win), 1)
    down = jnp.sum(jnp.where(earlier == later, across, 0), axis=1, keepdims=True)
    same = (across == down) & (earlier < later)
    rank = jnp.sum(same.astype(jnp.int32), axis=0, keepdims=True)
    return holder, rank


def pick_kernel(
    turn_ref,
    prob_ref,
    slot_ref,
    panel_ref,
    border_ref,
    inverse_ref,
    barrier_ref,
    first_ref,
    message_ref,
    put_ref,
    weight_ref,
    rounds_ref,
):
    rows_inv, rows_dev = border_ref.shape
    win = first_ref.shape[1]
    z_count = put_ref.shape[0]
    weight_ref[...] = jnp.full(weight_ref.shape, prob_ref[slot_ref[0]], F32)
    panel_row = panel_ref[...][None, :]
    holder, rank = places(panel_row, 2 * rows_dev, z_count)
    rounds_ref[0] = jnp.max(rank) + 1
    place = rank - turn_ref[0] * SLOTS
    local = panel_row - my_row() * rows_dev
    in_slot = place == iota((SLOTS, win), 0)
    mine = in_slot & (local >= 0) & (local < rows_dev)
    source = jnp.sum(jnp.where(mine, local + 1, 0), axis=1, keepdims=True) - 1
    pick = (source == iota((SLOTS, rows_dev), 1)).astype(F32).astype(BF16)
    picked = contract(pick, border_ref[...], 1, 1)
    for z in range(z_count):
        put_ref[z] = jnp.where(in_slot & (holder == z), 1.0, 0.0).astype(BF16)
    share = win // lax.axis_size(SCEN)
    at = lax.axis_index(SCEN) * share + iota((share, win), 0)
    on_diagonal = at == iota((share, win), 1)
    own = jnp.sum(jnp.where(on_diagonal, local, 0), axis=1, keepdims=True)
    hit = own == iota((share, rows_dev), 1)
    base = contract(hit.astype(F32), first_ref[...], 1, 0, HIGHEST)
    term = jnp.sum(jnp.where(hit, barrier_ref[...][None, :], 0.0), axis=1, keepdims=True)
    base = base + jnp.where(on_diagonal, term, 0.0)
    rounded = base.astype(BF16).astype(F32)
    fold = rows_inv // win
    step = share // fold
    lanes = [
        jnp.concatenate([part[step * i : step * (i + 1)] for i in range(fold)], axis=1)
        for part in (rounded, base - rounded)
    ]
    lines = [*lanes, inverse_ref[...].astype(F32), picked]
    message_ref[...] = jnp.concatenate(lines, axis=0).astype(BF16)


def gather_round(turn, border, inverse_rows, first_section, barrier, panel_vars, prob, slot):
    rows_inv, rows_dev = border.shape
    win = panel_vars.shape[0]
    z_count = lax.axis_size("z")
    extra = 2 * win // lax.axis_size(SCEN) * win // rows_inv
    vmem = pl.BlockSpec(memory_space=pltpu.VMEM)
    smem = pl.BlockSpec(memory_space=pltpu.SMEM)
    message, put, weight, most = pl.pallas_call(
        pick_kernel,
        out_shape=(
            jax.ShapeDtypeStruct((extra + inverse_rows.shape[0] + SLOTS, rows_inv), BF16),
            jax.ShapeDtypeStruct((z_count, SLOTS, win), BF16),
            jax.ShapeDtypeStruct((1, win), F32),
            jax.ShapeDtypeStruct((1,), jnp.int32),
        ),
        in_specs=[smem, smem, smem, vmem, vmem, vmem, vmem, vmem],
        out_specs=(vmem, vmem, vmem, smem),
        compiler_params=LIMIT,
    )(turn, prob, slot, panel_vars, border, inverse_rows, barrier, first_section)
    both = lax.all_gather(message, "xh", axis=0)
    mine = both[0, -SLOTS:] + both[1, -SLOTS:]
    everyone = lax.all_gather(mine, "z", axis=0)
    columns = lax.dot_general(
        everyone, put, (((0, 1), (0, 1)), ((), ())), preferred_element_type=F32
    ).astype(BF16)
    return columns, most[0], both[:, :-SLOTS], weight


def solve_kernel(both_ref, columns_ref, out_ref):
    _, lines, rows_inv = both_ref.shape
    win = columns_ref.shape[1]
    own = rows_inv // (2 * lax.axis_size("z"))
    extra = lines - own
    both = both_ref[...].astype(F32)
    rows = both[:, extra:, :].reshape(2 * own, rows_inv).astype(BF16)
    solved = contract(rows, columns_ref[...], 1, 0)
    parts = both[0, :extra, :] + both[1, :extra, :]
    fold = rows_inv // win
    step = extra // 2
    lanes = [
        parts[step * p : step * (p + 1), win * i : win * (i + 1)] for p in range(2) for i in range(fold)
    ]
    out_ref[...] = jnp.concatenate([solved, *lanes], axis=0).astype(BF16)


def term_kernel(columns_ref, border_ref, gathered_ref, weight_ref, keep_ref, give_ref, base_ref):
    z_count, lines, win = gathered_ref.shape
    rows_inv = border_ref.shape[0]
    chips, per_scen, _ = keep_ref.shape
    share = base_ref.shape[0]
    step = rows_inv // z_count
    solved = gathered_ref[:, :step, :].reshape(rows_inv, win)
    weight = weight_ref[...]
    block = contract(columns_ref[...], solved, 0, 0) * weight
    block = block.reshape(chips, 2, share, win)
    term = contract(border_ref[...], solved, 0, 0) * weight
    term = term.reshape(chips, 2, per_scen - share, win)
    for core in range(2):

        @pl.when(lax.axis_index("core") == core)
        def _(core=core):
            keep_ref[:, :share, :] = block[:, core]
            keep_ref[:, share:, :] = term[:, core]
            give_ref[:, :share, :] = block[:, 1 - core]
            give_ref[:, share:, :] = term[:, 1 - core]

    parts = jnp.sum(gathered_ref[:, step:, :].astype(F32), axis=0)
    base_ref[...] = parts[:share] + parts[share:]


def tree_sum(terms):
    while len(terms) > 1:
        terms = [sum(terms[i : i + 2][1:], terms[i]) for i in range(0, len(terms), 2)]
    return terms[0]


def inverse_factor(symmetric):
    size = symmetric.shape[0]
    count = size // GROUP
    shape = (GROUP, size)
    work = [symmetric[GROUP * i : GROUP * (i + 1), :] for i in range(count)]
    lane, sub = iota(shape, 1), iota(shape, 0)
    result = []
    for group in range(count):
        low = group * GROUP
        block = work[group]
        inside = (lane >= low) & (lane < low + GROUP)
        entry = [
            [jnp.broadcast_to(block[i : i + 1, low + j : low + j + 1], shape) for j in range(i + 1)]
            for i in range(GROUP)
        ]
        pivot = [None] * GROUP
        lower = [[None] * GROUP for _ in range(GROUP)]
        for j in range(GROUP):
            pivot[j] = 1.0 / entry[j][j]
            for i in range(j + 1, GROUP):
                lower[i][j] = entry[i][j] * pivot[j]
            for i in range(j + 1, GROUP):
                for t in range(j + 1, i + 1):
                    entry[i][t] = entry[i][t] - (entry[i][j] * entry[t][j]) * pivot[j]
        unit = [[None] * GROUP for _ in range(GROUP)]
        for i in range(GROUP):
            for j in range(i):
                value = lower[i][j]
                for t in range(j + 1, i):
                    value = value + lower[i][t] * unit[t][j]
                unit[i][j] = -value
        rows = jnp.where(inside, jnp.where(lane == sub + low, 1.0, 0.0), block)
        spots = [jnp.broadcast_to(rows[j : j + 1, :], shape) for j in range(GROUP)]
        forward = [
            tree_sum([spots[i]] + [unit[i][j] * spots[j] for j in range(i)]) for i in range(GROUP)
        ]
        done, scale = forward[0], pivot[0]
        for i in range(1, GROUP):
            done = jnp.where(sub == i, forward[i], done)
            scale = jnp.where(sub == i, pivot[i], scale)
        result.append(jnp.where(lane <= sub + low, done * jnp.sqrt(scale), 0.0))
        if group + 1 == count:
            break
        scaled = [forward[i] * pivot[i] for i in range(GROUP)]
        back = [
            tree_sum([scaled[j]] + [unit[i][j] * scaled[i] for i in range(j + 1, GROUP)])
            for j in range(GROUP)
        ]
        near = group + 2 if count - group > 4 else count
        for later in range(group + 1, near):
            old = work[later]
            taken = tree_sum([old[:, low + j : low + j + 1] * back[j] for j in range(GROUP)])
            work[later] = jnp.where(inside, 0.0, old) - taken
        if near < count:
            stacked = back[0]
            for j in range(1, GROUP):
                stacked = jnp.where(sub == j, back[j], stacked)
            zero = jnp.zeros(shape, F32)
            spread = [stacked if i == group else zero for i in range(count)]
            taken = contract_split(
                jnp.concatenate(work[near:], axis=0), jnp.concatenate(spread, axis=0), 1, 0
            )
            for later in range(near, count):
                at = GROUP * (later - near)
                work[later] = jnp.where(inside, 0.0, work[later]) - taken[at : at + GROUP]
    return jnp.concatenate(result, axis=0)


def factor_kernel(gathered_ref, base_ref, out_ref):
    cores, chips, per_scen, win = gathered_ref.shape
    share = win // (cores * chips)
    order = [(core, chip) for chip in range(chips) for core in range(cores)]
    diag = jnp.concatenate([gathered_ref[core, chip, :share, :] for core, chip in order], axis=0)
    rows = jnp.concatenate([gathered_ref[core, chip, share:, :] for core, chip in order], axis=0)
    rows = rows + base_ref[...]

    def symmetric(i, j):
        one = diag[i : i + PANEL, j : j + PANEL]
        other = diag[j : j + PANEL, i : i + PANEL]
        return 0.5 * (one + other.T)

    first = inverse_factor(symmetric(0, 0))
    across = contract_split(symmetric(PANEL, 0), first, 1, 1)
    second = inverse_factor(symmetric(PANEL, PANEL) - contract_split(across, across, 1, 1))
    left = contract_split(rows[:, :PANEL], first, 1, 1)
    right = rows[:, PANEL:] - contract_split(left, across, 1, 1)
    out_ref[:, :PANEL] = left
    out_ref[:, PANEL:] = contract_split(right, second, 1, 1)


def per_device(borders, kkt_inverse, first_section, barrier, panel_vars, probability, assignment):
    border, inverse_rows = borders[0], kkt_inverse[0]
    rows_inv, rows_dev = border.shape
    win = first_section.shape[1]
    scen_count = lax.axis_size(SCEN)
    share = win // scen_count

    def turn(number):
        return gather_round(
            number[None],
            border,
            inverse_rows,
            first_section,
            barrier,
            panel_vars,
            probability,
            assignment,
        )

    columns, most, both, weight = turn(jnp.int32(0))
    _, columns = lax.while_loop(
        lambda state: state[0] * SLOTS < most,
        lambda state: (state[0] + 1, state[1] + turn(state[0])[0]),
        (jnp.int32(1), columns),
    )

    own_lines = 2 * inverse_rows.shape[0]
    message = pl.pallas_call(
        solve_kernel,
        out_shape=jax.ShapeDtypeStruct((own_lines + 2 * share, win), BF16),
        compiler_params=LIMIT,
    )(both, columns)
    gathered = lax.all_gather(message, "z", axis=0)

    per_scen = share + rows_dev // scen_count
    half = jax.ShapeDtypeStruct((lax.axis_size("chip"), per_scen, win), F32)
    keep, give, base = pl.pallas_call(
        term_kernel,
        out_shape=(half, half, jax.ShapeDtypeStruct((share, win), F32)),
        compiler_params=LIMIT,
    )(columns, border, gathered, weight)
    given = lax.all_gather(give, "core", axis=0)
    pair = keep + lax.dynamic_index_in_dim(given, 1 - lax.axis_index("core"), 0, keepdims=False)
    shares = lax.all_to_all(pair, "chip", 0, 0, tiled=True)
    total = jnp.sum(shares, axis=0) + jnp.pad(base, ((0, per_scen - share), (0, 0)))
    copies = jnp.broadcast_to(total[None], half.shape)
    everyone = lax.all_to_all(copies, "chip", 0, 0, tiled=True)
    everyone = lax.all_gather(everyone, "core", axis=0)

    hits = (
        jnp.arange(rows_dev, dtype=jnp.int32)[:, None] + my_row() * rows_dev == panel_vars[None, :]
    )
    rows_base = first_section + jnp.where(hits, barrier[:, None], 0.0)
    return pl.pallas_call(
        factor_kernel,
        out_shape=jax.ShapeDtypeStruct((rows_dev, win), F32),
        compiler_params=LIMIT,
    )(everyone, rows_base)


def solution(mesh):
    torus = Mesh(mesh.devices.reshape(8, 2, 16, 2), (*SCEN, *ROW))
    return jax.shard_map(
        per_device,
        mesh=torus,
        in_specs=(
            P(SCEN, None, ROW),
            P(SCEN, ROW, None),
            P(ROW, None),
            P(ROW),
            P(),
            P(),
            P(SCEN),
        ),
        out_specs=P(ROW, None),
        check_vma=False,
    )
```

```python
import jax
import jax.numpy as jnp
from jax import lax
from jax.experimental import pallas as pl
from jax.experimental.pallas import tpu as pltpu
from jax.sharding import Mesh
from jax.sharding import PartitionSpec as P

SLOTS = 31
GROUP = 8
PANEL = 128
ROW = ("z", "xh")
SCEN = ("chip", "core")
F32 = jnp.float32
BF16 = jnp.bfloat16
LIMIT = pltpu.CompilerParams(vmem_limit_bytes=48 * 1024 * 1024)


def iota(shape, dim):
    return lax.broadcasted_iota(jnp.int32, shape, dim)


def contract(a, b, dim_a, dim_b):
    return lax.dot_general(a, b, (((dim_a,), (dim_b,)), ((), ())), preferred_element_type=F32)


def contract_split(a, b, dim_a, dim_b):
    a_high, b_high = a.astype(BF16), b.astype(BF16)
    a_low = (a - a_high.astype(F32)).astype(BF16)
    b_low = (b - b_high.astype(F32)).astype(BF16)
    small = contract(a_high, b_low, dim_a, dim_b) + contract(a_low, b_high, dim_a, dim_b)
    return contract(a_high, b_high, dim_a, dim_b) + small


def my_row():
    return lax.axis_index("z") * 2 + lax.axis_index("xh")


def places(panel_row, rows_pair, holders):
    win = panel_row.shape[1]
    holder = jnp.zeros_like(panel_row)
    for z in range(1, holders):
        holder = holder + (panel_row >= z * rows_pair).astype(jnp.int32)
    across = jnp.broadcast_to(holder, (win, win))
    earlier, later = iota((win, win), 0), iota((win, win), 1)
    down = jnp.sum(jnp.where(earlier == later, across, 0), axis=1, keepdims=True)
    same = (across == down) & (earlier < later)
    rank = jnp.sum(same.astype(jnp.int32), axis=0, keepdims=True)
    return holder, rank


def pick_kernel(
    turn_ref,
    prob_ref,
    slot_ref,
    panel_ref,
    border_ref,
    inverse_ref,
    barrier_ref,
    first_ref,
    message_ref,
    put_ref,
    weight_ref,
    rounds_ref,
):
    rows_inv, rows_dev = border_ref.shape
    win = first_ref.shape[1]
    z_count = put_ref.shape[0]
    weight_ref[...] = jnp.full(weight_ref.shape, prob_ref[slot_ref[0]], F32)
    panel_row = panel_ref[...][None, :]
    holder, rank = places(panel_row, 2 * rows_dev, z_count)
    rounds_ref[0] = jnp.max(rank) + 1
    place = rank - turn_ref[0] * SLOTS
    local = panel_row - my_row() * rows_dev
    in_slot = place == iota((SLOTS, win), 0)
    mine = in_slot & (local >= 0) & (local < rows_dev)
    source = jnp.sum(jnp.where(mine, local + 1, 0), axis=1, keepdims=True) - 1
    pick = (source == iota((SLOTS, rows_dev), 1)).astype(F32).astype(BF16)
    picked = contract(pick, border_ref[...], 1, 1)
    for z in range(z_count):
        put_ref[z] = jnp.where(in_slot & (holder == z), 1.0, 0.0).astype(BF16)
    share = win // lax.axis_size(SCEN)
    at = lax.axis_index(SCEN) * share + iota((share, win), 0)
    on_diagonal = at == iota((share, win), 1)
    own = jnp.sum(jnp.where(on_diagonal, local, 0), axis=1, keepdims=True)
    hit = own == iota((share, rows_dev), 1)
    first = first_ref[...]
    first_high = first.astype(BF16)
    first_low = (first - first_high.astype(F32)).astype(BF16)
    pick = hit.astype(F32).astype(BF16)
    base = contract(pick, first_high, 1, 0) + contract(pick, first_low, 1, 0)
    term = jnp.sum(jnp.where(hit, barrier_ref[...][None, :], 0.0), axis=1, keepdims=True)
    base = base + jnp.where(on_diagonal, term, 0.0)
    rounded = base.astype(BF16).astype(F32)
    fold = rows_inv // win
    step = share // fold
    lanes = [
        jnp.concatenate([part[step * i : step * (i + 1)] for i in range(fold)], axis=1)
        for part in (rounded, base - rounded)
    ]
    lines = [*lanes, inverse_ref[...].astype(F32), picked]
    message_ref[...] = jnp.concatenate(lines, axis=0).astype(BF16)


def gather_round(turn, border, inverse_rows, first_section, barrier, panel_vars, prob, slot):
    rows_inv, rows_dev = border.shape
    win = panel_vars.shape[0]
    z_count = lax.axis_size("z")
    extra = 2 * win // lax.axis_size(SCEN) * win // rows_inv
    vmem = pl.BlockSpec(memory_space=pltpu.VMEM)
    smem = pl.BlockSpec(memory_space=pltpu.SMEM)
    message, put, weight, most = pl.pallas_call(
        pick_kernel,
        out_shape=(
            jax.ShapeDtypeStruct((extra + inverse_rows.shape[0] + SLOTS, rows_inv), BF16),
            jax.ShapeDtypeStruct((z_count, SLOTS, win), BF16),
            jax.ShapeDtypeStruct((1, win), F32),
            jax.ShapeDtypeStruct((1,), jnp.int32),
        ),
        in_specs=[smem, smem, smem, vmem, vmem, vmem, vmem, vmem],
        out_specs=(vmem, vmem, vmem, smem),
        compiler_params=LIMIT,
    )(turn, prob, slot, panel_vars, border, inverse_rows, barrier, first_section)
    both = lax.all_gather(message, "xh", axis=0)
    mine = both[0, -SLOTS:] + both[1, -SLOTS:]
    everyone = lax.all_gather(mine, "z", axis=0)
    columns = lax.dot_general(
        everyone, put, (((0, 1), (0, 1)), ((), ())), preferred_element_type=F32
    ).astype(BF16)
    return columns, most[0], both[:, :-SLOTS], weight


def solve_kernel(both_ref, columns_ref, out_ref):
    _, lines, rows_inv = both_ref.shape
    win = columns_ref.shape[1]
    own = rows_inv // (2 * lax.axis_size("z"))
    extra = lines - own
    both = both_ref[...].astype(F32)
    rows = both[:, extra:, :].reshape(2 * own, rows_inv).astype(BF16)
    solved = contract(rows, columns_ref[...], 1, 0)
    parts = both[0, :extra, :] + both[1, :extra, :]
    fold = rows_inv // win
    step = extra // 2
    lanes = [
        parts[step * p : step * (p + 1), win * i : win * (i + 1)] for p in range(2) for i in range(fold)
    ]
    out_ref[...] = jnp.concatenate([solved, *lanes], axis=0).astype(BF16)


def term_kernel(columns_ref, border_ref, gathered_ref, weight_ref, keep_ref, give_ref, base_ref):
    z_count, lines, win = gathered_ref.shape
    rows_inv = border_ref.shape[0]
    chips, per_scen, _ = keep_ref.shape
    share = base_ref.shape[0]
    step = rows_inv // z_count
    solved = gathered_ref[:, :step, :].reshape(rows_inv, win)
    weight = weight_ref[...]
    block = contract(columns_ref[...], solved, 0, 0) * weight
    block = block.reshape(chips, 2, share, win)
    term = contract(border_ref[...], solved, 0, 0) * weight
    term = term.reshape(chips, 2, per_scen - share, win)
    for core in range(2):

        @pl.when(lax.axis_index("core") == core)
        def _(core=core):
            keep_ref[:, :share, :] = block[:, core]
            keep_ref[:, share:, :] = term[:, core]
            give_ref[:, :share, :] = block[:, 1 - core]
            give_ref[:, share:, :] = term[:, 1 - core]

    parts = jnp.sum(gathered_ref[:, step:, :].astype(F32), axis=0)
    base_ref[...] = parts[:share] + parts[share:]


def tree_sum(terms):
    while len(terms) > 1:
        terms = [sum(terms[i : i + 2][1:], terms[i]) for i in range(0, len(terms), 2)]
    return terms[0]


def inverse_factor(symmetric):
    size = symmetric.shape[0]
    count = size // GROUP
    shape = (GROUP, size)
    work = [symmetric[GROUP * i : GROUP * (i + 1), :] for i in range(count)]
    lane, sub = iota(shape, 1), iota(shape, 0)
    result = []
    for group in range(count):
        low = group * GROUP
        block = work[group]
        inside = (lane >= low) & (lane < low + GROUP)
        entry = [
            [jnp.broadcast_to(block[i : i + 1, low + j : low + j + 1], shape) for j in range(i + 1)]
            for i in range(GROUP)
        ]
        pivot = [None] * GROUP
        lower = [[None] * GROUP for _ in range(GROUP)]
        for j in range(GROUP):
            pivot[j] = 1.0 / entry[j][j]
            for i in range(j + 1, GROUP):
                lower[i][j] = entry[i][j] * pivot[j]
            for i in range(j + 1, GROUP):
                for t in range(j + 1, i + 1):
                    entry[i][t] = entry[i][t] - (entry[i][j] * entry[t][j]) * pivot[j]
        unit = [[None] * GROUP for _ in range(GROUP)]
        for i in range(GROUP):
            for j in range(i):
                value = lower[i][j]
                for t in range(j + 1, i):
                    value = value + lower[i][t] * unit[t][j]
                unit[i][j] = -value
        rows = jnp.where(inside, jnp.where(lane == sub + low, 1.0, 0.0), block)
        spots = [jnp.broadcast_to(rows[j : j + 1, :], shape) for j in range(GROUP)]
        forward = [
            tree_sum([spots[i]] + [unit[i][j] * spots[j] for j in range(i)]) for i in range(GROUP)
        ]
        done, scale = forward[0], pivot[0]
        for i in range(1, GROUP):
            done = jnp.where(sub == i, forward[i], done)
            scale = jnp.where(sub == i, pivot[i], scale)
        result.append(jnp.where(lane <= sub + low, done * jnp.sqrt(scale), 0.0))
        if group + 1 == count:
            break
        scaled = [forward[i] * pivot[i] for i in range(GROUP)]
        back = [
            tree_sum([scaled[j]] + [unit[i][j] * scaled[i] for i in range(j + 1, GROUP)])
            for j in range(GROUP)
        ]
        near = group + 2 if count - group > 4 else count
        for later in range(group + 1, near):
            old = work[later]
            taken = tree_sum([old[:, low + j : low + j + 1] * back[j] for j in range(GROUP)])
            work[later] = jnp.where(inside, 0.0, old) - taken
        if near < count:
            stacked = back[0]
            for j in range(1, GROUP):
                stacked = jnp.where(sub == j, back[j], stacked)
            zero = jnp.zeros(shape, F32)
            spread = [stacked if i == group else zero for i in range(count)]
            taken = contract_split(
                jnp.concatenate(work[near:], axis=0), jnp.concatenate(spread, axis=0), 1, 0
            )
            for later in range(near, count):
                at = GROUP * (later - near)
                work[later] = jnp.where(inside, 0.0, work[later]) - taken[at : at + GROUP]
    return jnp.concatenate(result, axis=0)


def factor_kernel(gathered_ref, base_ref, out_ref):
    cores, chips, per_scen, win = gathered_ref.shape
    share = win // (cores * chips)
    order = [(core, chip) for chip in range(chips) for core in range(cores)]
    diag = jnp.concatenate([gathered_ref[core, chip, :share, :] for core, chip in order], axis=0)
    rows = jnp.concatenate([gathered_ref[core, chip, share:, :] for core, chip in order], axis=0)
    rows = rows + base_ref[...]

    def symmetric(i, j):
        one = diag[i : i + PANEL, j : j + PANEL]
        other = diag[j : j + PANEL, i : i + PANEL]
        return 0.5 * (one + other.T)

    first = inverse_factor(symmetric(0, 0))
    across = contract_split(symmetric(PANEL, 0), first, 1, 1)
    second = inverse_factor(symmetric(PANEL, PANEL) - contract_split(across, across, 1, 1))
    left = contract_split(rows[:, :PANEL], first, 1, 1)
    right = rows[:, PANEL:] - contract_split(left, across, 1, 1)
    out_ref[:, :PANEL] = left
    out_ref[:, PANEL:] = contract_split(right, second, 1, 1)


def per_device(borders, kkt_inverse, first_section, barrier, panel_vars, probability, assignment):
    border, inverse_rows = borders[0], kkt_inverse[0]
    rows_inv, rows_dev = border.shape
    win = first_section.shape[1]
    scen_count = lax.axis_size(SCEN)
    share = win // scen_count

    def turn(number):
        return gather_round(
            number[None],
            border,
            inverse_rows,
            first_section,
            barrier,
            panel_vars,
            probability,
            assignment,
        )

    columns, most, both, weight = turn(jnp.int32(0))
    _, columns = lax.while_loop(
        lambda state: state[0] * SLOTS < most,
        lambda state: (state[0] + 1, state[1] + turn(state[0])[0]),
        (jnp.int32(1), columns),
    )

    own_lines = 2 * inverse_rows.shape[0]
    message = pl.pallas_call(
        solve_kernel,
        out_shape=jax.ShapeDtypeStruct((own_lines + 2 * share, win), BF16),
        compiler_params=LIMIT,
    )(both, columns)
    gathered = lax.all_gather(message, "z", axis=0)

    per_scen = share + rows_dev // scen_count
    half = jax.ShapeDtypeStruct((lax.axis_size("chip"), per_scen, win), F32)
    keep, give, base = pl.pallas_call(
        term_kernel,
        out_shape=(half, half, jax.ShapeDtypeStruct((share, win), F32)),
        compiler_params=LIMIT,
    )(columns, border, gathered, weight)
    given = lax.all_gather(give, "core", axis=0)
    pair = keep + lax.dynamic_index_in_dim(given, 1 - lax.axis_index("core"), 0, keepdims=False)
    shares = lax.all_to_all(pair, "chip", 0, 0, tiled=True)
    total = jnp.sum(shares, axis=0) + jnp.pad(base, ((0, per_scen - share), (0, 0)))
    copies = jnp.broadcast_to(total[None], half.shape)
    everyone = lax.all_to_all(copies, "chip", 0, 0, tiled=True)
    everyone = lax.all_gather(everyone, "core", axis=0)

    hits = (
        jnp.arange(rows_dev, dtype=jnp.int32)[:, None] + my_row() * rows_dev == panel_vars[None, :]
    )
    rows_base = first_section + jnp.where(hits, barrier[:, None], 0.0)
    return pl.pallas_call(
        factor_kernel,
        out_shape=jax.ShapeDtypeStruct((rows_dev, win), F32),
        compiler_params=LIMIT,
    )(everyone, rows_base)


def solution(mesh):
    torus = Mesh(mesh.devices.reshape(8, 2, 16, 2), (*SCEN, *ROW))
    return jax.shard_map(
        per_device,
        mesh=torus,
        in_specs=(
            P(SCEN, None, ROW),
            P(SCEN, ROW, None),
            P(ROW, None),
            P(ROW),
            P(),
            P(),
            P(SCEN),
        ),
        out_specs=P(ROW, None),
        check_vma=False,
    )
```

```python
import jax
import jax.numpy as jnp
from jax import lax
from jax.experimental import pallas as pl
from jax.experimental.pallas import tpu as pltpu
from jax.sharding import Mesh
from jax.sharding import PartitionSpec as P

SLOTS = 31
GROUP = 8
PANEL = 128
ROW = ("z", "xh")
SCEN = ("chip", "core")
F32 = jnp.float32
BF16 = jnp.bfloat16
LIMIT = pltpu.CompilerParams(vmem_limit_bytes=48 * 1024 * 1024)


def iota(shape, dim):
    return lax.broadcasted_iota(jnp.int32, shape, dim)


def contract(a, b, dim_a, dim_b):
    return lax.dot_general(a, b, (((dim_a,), (dim_b,)), ((), ())), preferred_element_type=F32)


def contract_split(a, b, dim_a, dim_b):
    a_high, b_high = a.astype(BF16), b.astype(BF16)
    a_low = (a - a_high.astype(F32)).astype(BF16)
    b_low = (b - b_high.astype(F32)).astype(BF16)
    small = contract(a_high, b_low, dim_a, dim_b) + contract(a_low, b_high, dim_a, dim_b)
    return contract(a_high, b_high, dim_a, dim_b) + small


def my_row():
    return lax.axis_index("z") * 2 + lax.axis_index("xh")


def places(panel_row, rows_pair, holders):
    win = panel_row.shape[1]
    holder = jnp.zeros_like(panel_row)
    for z in range(1, holders):
        holder = holder + (panel_row >= z * rows_pair).astype(jnp.int32)
    across = jnp.broadcast_to(holder.astype(F32), (win, win))
    earlier, later = iota((win, win), 0), iota((win, win), 1)
    down = jnp.sum(jnp.where(earlier == later, across, 0.0), axis=1, keepdims=True)
    same = (across == down) & (earlier < later)
    rank = jnp.sum(same.astype(F32), axis=0, keepdims=True).astype(jnp.int32)
    return holder, rank


def pick_kernel(
    turn_ref,
    prob_ref,
    slot_ref,
    panel_ref,
    border_ref,
    inverse_ref,
    barrier_ref,
    first_ref,
    message_ref,
    put_ref,
    weight_ref,
    rounds_ref,
):
    rows_inv, rows_dev = border_ref.shape
    win = first_ref.shape[1]
    z_count = put_ref.shape[0]
    weight_ref[...] = jnp.full(weight_ref.shape, prob_ref[slot_ref[0]], F32)
    panel_row = panel_ref[...][None, :]
    holder, rank = places(panel_row, 2 * rows_dev, z_count)
    rounds_ref[0] = jnp.max(rank) + 1
    place = rank - turn_ref[0] * SLOTS
    local = panel_row - my_row() * rows_dev
    in_slot = place == iota((SLOTS, win), 0)
    mine = in_slot & (local >= 0) & (local < rows_dev)
    spot = jnp.where(mine, (local + 1).astype(F32), 0.0)
    source = jnp.sum(spot, axis=1, keepdims=True).astype(jnp.int32) - 1
    pick = (source == iota((SLOTS, rows_dev), 1)).astype(F32).astype(BF16)
    picked = contract(pick, border_ref[...], 1, 1)
    for z in range(z_count):
        put_ref[z] = jnp.where(in_slot & (holder == z), 1.0, 0.0).astype(BF16)
    share = win // lax.axis_size(SCEN)
    at = lax.axis_index(SCEN) * share + iota((share, win), 0)
    on_diagonal = at == iota((share, win), 1)
    own = jnp.where(on_diagonal, local.astype(F32), 0.0)
    own = jnp.sum(own, axis=1, keepdims=True).astype(jnp.int32)
    hit = own == iota((share, rows_dev), 1)
    first = first_ref[...]
    first_high = first.astype(BF16)
    first_low = (first - first_high.astype(F32)).astype(BF16)
    pick = hit.astype(F32).astype(BF16)
    base = contract(pick, first_high, 1, 0) + contract(pick, first_low, 1, 0)
    term = jnp.sum(jnp.where(hit, barrier_ref[...][None, :], 0.0), axis=1, keepdims=True)
    base = base + jnp.where(on_diagonal, term, 0.0)
    rounded = base.astype(BF16).astype(F32)
    fold = rows_inv // win
    step = share // fold
    lanes = [
        jnp.concatenate([part[step * i : step * (i + 1)] for i in range(fold)], axis=1)
        for part in (rounded, base - rounded)
    ]
    lines = [*lanes, inverse_ref[...].astype(F32), picked]
    message_ref[...] = jnp.concatenate(lines, axis=0).astype(BF16)


def gather_round(turn, border, inverse_rows, first_section, barrier, panel_vars, prob, slot):
    rows_inv, rows_dev = border.shape
    win = panel_vars.shape[0]
    z_count = lax.axis_size("z")
    extra = 2 * win // lax.axis_size(SCEN) * win // rows_inv
    vmem = pl.BlockSpec(memory_space=pltpu.VMEM)
    smem = pl.BlockSpec(memory_space=pltpu.SMEM)
    message, put, weight, most = pl.pallas_call(
        pick_kernel,
        out_shape=(
            jax.ShapeDtypeStruct((extra + inverse_rows.shape[0] + SLOTS, rows_inv), BF16),
            jax.ShapeDtypeStruct((z_count, SLOTS, win), BF16),
            jax.ShapeDtypeStruct((1, win), F32),
            jax.ShapeDtypeStruct((1,), jnp.int32),
        ),
        in_specs=[smem, smem, smem, vmem, vmem, vmem, vmem, vmem],
        out_specs=(vmem, vmem, vmem, smem),
        compiler_params=LIMIT,
    )(turn, prob, slot, panel_vars, border, inverse_rows, barrier, first_section)
    both = lax.all_gather(message, "xh", axis=0)
    mine = both[0, -SLOTS:] + both[1, -SLOTS:]
    everyone = lax.all_gather(mine, "z", axis=0)
    columns = lax.dot_general(
        everyone, put, (((0, 1), (0, 1)), ((), ())), preferred_element_type=F32
    ).astype(BF16)
    return columns, most[0], both[:, :-SLOTS], weight


def solve_kernel(both_ref, columns_ref, out_ref):
    _, lines, rows_inv = both_ref.shape
    win = columns_ref.shape[1]
    own = rows_inv // (2 * lax.axis_size("z"))
    extra = lines - own
    both = both_ref[...].astype(F32)
    rows = both[:, extra:, :].reshape(2 * own, rows_inv).astype(BF16)
    solved = contract(rows, columns_ref[...], 1, 0)
    parts = both[0, :extra, :] + both[1, :extra, :]
    fold = rows_inv // win
    step = extra // 2
    lanes = [
        parts[step * p : step * (p + 1), win * i : win * (i + 1)] for p in range(2) for i in range(fold)
    ]
    out_ref[...] = jnp.concatenate([solved, *lanes], axis=0).astype(BF16)


def term_kernel(columns_ref, border_ref, gathered_ref, weight_ref, keep_ref, give_ref, base_ref):
    z_count, lines, win = gathered_ref.shape
    rows_inv = border_ref.shape[0]
    chips, per_scen, _ = keep_ref.shape
    share = base_ref.shape[0]
    step = rows_inv // z_count
    solved = gathered_ref[:, :step, :].reshape(rows_inv, win)
    weight = weight_ref[...]
    block = contract(columns_ref[...], solved, 0, 0) * weight
    block = block.reshape(chips, 2, share, win)
    term = contract(border_ref[...], solved, 0, 0) * weight
    term = term.reshape(chips, 2, per_scen - share, win)
    for core in range(2):

        @pl.when(lax.axis_index("core") == core)
        def _(core=core):
            keep_ref[:, :share, :] = block[:, core]
            keep_ref[:, share:, :] = term[:, core]
            give_ref[:, :share, :] = block[:, 1 - core]
            give_ref[:, share:, :] = term[:, 1 - core]

    parts = jnp.sum(gathered_ref[:, step:, :].astype(F32), axis=0)
    base_ref[...] = parts[:share] + parts[share:]


def tree_sum(terms):
    while len(terms) > 1:
        terms = [sum(terms[i : i + 2][1:], terms[i]) for i in range(0, len(terms), 2)]
    return terms[0]


def inverse_factor(symmetric):
    size = symmetric.shape[0]
    count = size // GROUP
    shape = (GROUP, size)
    work = [symmetric[GROUP * i : GROUP * (i + 1), :] for i in range(count)]
    lane, sub = iota(shape, 1), iota(shape, 0)
    result = []
    for group in range(count):
        low = group * GROUP
        block = work[group]
        inside = (lane >= low) & (lane < low + GROUP)
        entry = [
            [jnp.broadcast_to(block[i : i + 1, low + j : low + j + 1], shape) for j in range(i + 1)]
            for i in range(GROUP)
        ]
        pivot = [None] * GROUP
        lower = [[None] * GROUP for _ in range(GROUP)]
        for j in range(GROUP):
            pivot[j] = 1.0 / entry[j][j]
            for i in range(j + 1, GROUP):
                lower[i][j] = entry[i][j] * pivot[j]
            for i in range(j + 1, GROUP):
                for t in range(j + 1, i + 1):
                    entry[i][t] = entry[i][t] - (entry[i][j] * entry[t][j]) * pivot[j]
        unit = [[None] * GROUP for _ in range(GROUP)]
        for i in range(GROUP):
            for j in range(i):
                value = lower[i][j]
                for t in range(j + 1, i):
                    value = value + lower[i][t] * unit[t][j]
                unit[i][j] = -value
        rows = jnp.where(inside, jnp.where(lane == sub + low, 1.0, 0.0), block)
        spots = [jnp.broadcast_to(rows[j : j + 1, :], shape) for j in range(GROUP)]
        forward = [
            tree_sum([spots[i]] + [unit[i][j] * spots[j] for j in range(i)]) for i in range(GROUP)
        ]
        done, scale = forward[0], pivot[0]
        for i in range(1, GROUP):
            done = jnp.where(sub == i, forward[i], done)
            scale = jnp.where(sub == i, pivot[i], scale)
        result.append(jnp.where(lane <= sub + low, done * jnp.sqrt(scale), 0.0))
        if group + 1 == count:
            break
        scaled = [forward[i] * pivot[i] for i in range(GROUP)]
        back = [
            tree_sum([scaled[j]] + [unit[i][j] * scaled[i] for i in range(j + 1, GROUP)])
            for j in range(GROUP)
        ]
        near = group + 2 if count - group > 4 else count
        for later in range(group + 1, near):
            old = work[later]
            taken = tree_sum([old[:, low + j : low + j + 1] * back[j] for j in range(GROUP)])
            work[later] = jnp.where(inside, 0.0, old) - taken
        if near < count:
            stacked = back[0]
            for j in range(1, GROUP):
                stacked = jnp.where(sub == j, back[j], stacked)
            zero = jnp.zeros(shape, F32)
            spread = [stacked if i == group else zero for i in range(count)]
            taken = contract_split(
                jnp.concatenate(work[near:], axis=0), jnp.concatenate(spread, axis=0), 1, 0
            )
            for later in range(near, count):
                at = GROUP * (later - near)
                work[later] = jnp.where(inside, 0.0, work[later]) - taken[at : at + GROUP]
    return jnp.concatenate(result, axis=0)


def factor_kernel(gathered_ref, base_ref, out_ref):
    cores, chips, per_scen, win = gathered_ref.shape
    share = win // (cores * chips)
    order = [(core, chip) for chip in range(chips) for core in range(cores)]
    diag = jnp.concatenate([gathered_ref[core, chip, :share, :] for core, chip in order], axis=0)
    rows = jnp.concatenate([gathered_ref[core, chip, share:, :] for core, chip in order], axis=0)
    rows = rows + base_ref[...]

    def symmetric(i, j):
        one = diag[i : i + PANEL, j : j + PANEL]
        other = diag[j : j + PANEL, i : i + PANEL]
        return 0.5 * (one + other.T)

    first = inverse_factor(symmetric(0, 0))
    across = contract_split(symmetric(PANEL, 0), first, 1, 1)
    second = inverse_factor(symmetric(PANEL, PANEL) - contract_split(across, across, 1, 1))
    left = contract_split(rows[:, :PANEL], first, 1, 1)
    right = rows[:, PANEL:] - contract_split(left, across, 1, 1)
    out_ref[:, :PANEL] = left
    out_ref[:, PANEL:] = contract_split(right, second, 1, 1)


def per_device(borders, kkt_inverse, first_section, barrier, panel_vars, probability, assignment):
    border, inverse_rows = borders[0], kkt_inverse[0]
    rows_inv, rows_dev = border.shape
    win = first_section.shape[1]
    scen_count = lax.axis_size(SCEN)
    share = win // scen_count

    def turn(number):
        return gather_round(
            number[None],
            border,
            inverse_rows,
            first_section,
            barrier,
            panel_vars,
            probability,
            assignment,
        )

    columns, most, both, weight = turn(jnp.int32(0))
    _, columns = lax.while_loop(
        lambda state: state[0] * SLOTS < most,
        lambda state: (state[0] + 1, state[1] + turn(state[0])[0]),
        (jnp.int32(1), columns),
    )

    own_lines = 2 * inverse_rows.shape[0]
    message = pl.pallas_call(
        solve_kernel,
        out_shape=jax.ShapeDtypeStruct((own_lines + 2 * share, win), BF16),
        compiler_params=LIMIT,
    )(both, columns)
    gathered = lax.all_gather(message, "z", axis=0)

    per_scen = share + rows_dev // scen_count
    half = jax.ShapeDtypeStruct((lax.axis_size("chip"), per_scen, win), F32)
    keep, give, base = pl.pallas_call(
        term_kernel,
        out_shape=(half, half, jax.ShapeDtypeStruct((share, win), F32)),
        compiler_params=LIMIT,
    )(columns, border, gathered, weight)
    given = lax.all_gather(give, "core", axis=0)
    pair = keep + lax.dynamic_index_in_dim(given, 1 - lax.axis_index("core"), 0, keepdims=False)
    shares = lax.all_to_all(pair, "chip", 0, 0, tiled=True)
    total = jnp.sum(shares, axis=0) + jnp.pad(base, ((0, per_scen - share), (0, 0)))
    copies = jnp.broadcast_to(total[None], half.shape)
    everyone = lax.all_to_all(copies, "chip", 0, 0, tiled=True)
    everyone = lax.all_gather(everyone, "core", axis=0)

    hits = (
        jnp.arange(rows_dev, dtype=jnp.int32)[:, None] + my_row() * rows_dev == panel_vars[None, :]
    )
    rows_base = first_section + jnp.where(hits, barrier[:, None], 0.0)
    return pl.pallas_call(
        factor_kernel,
        out_shape=jax.ShapeDtypeStruct((rows_dev, win), F32),
        compiler_params=LIMIT,
    )(everyone, rows_base)


def solution(mesh):
    torus = Mesh(mesh.devices.reshape(8, 2, 16, 2), (*SCEN, *ROW))
    return jax.shard_map(
        per_device,
        mesh=torus,
        in_specs=(
            P(SCEN, None, ROW),
            P(SCEN, ROW, None),
            P(ROW, None),
            P(ROW),
            P(),
            P(),
            P(SCEN),
        ),
        out_specs=P(ROW, None),
        check_vma=False,
    )
```
